256 devices in a mesh: dp: 2 (over core), span: 8 (over z), head: 16 (over x, y).
Axes of the slice: x: 4, y: 4, z: 8, core: 2. Of those that a mesh axis runs over, the one named last changes fastest.
Arguments:
- hidden_in: bfloat16 [8192, 4096], P(('dp', 'span'), 'head'), parts along dimension 0, may hold values from -6 to 6
- norm_gain: bfloat16 [4096], P('head'), may hold values from 0.099609375 to 1.8984375
- w_query: bfloat16 [4096, 4096], P(None, 'head'), may hold values from -0.375 to 0.375
- enc_states: bfloat16 [32768, 1024], P(('dp', 'span', 'head')), parts along dimension 0
- w_key: bfloat16 [1024, 4096], P(None, 'head'), may hold values from -0.1875 to 0.1875
- w_value: bfloat16 [1024, 4096], P(None, 'head'), may hold values from -0.1875 to 0.1875
- w_out: bfloat16 [4096, 4096], P('head'), may hold values from -0.5 to 0.5
- block_counts: int32 [16], P('dp'), parts along dimension 0, may hold values from 1 to 16, as said below
Outputs:
- cross_out: bfloat16 [8192, 4096], P(('dp', 'span'), 'head'), parts along dimension 0
The draws below stay inside these ranges and needn't reach their ends.
There are 2 independent parts, one for each index of `dp`. The reference program is written for one: setup_inputs(seed, part) draws one part's arguments, and reference() takes and returns one part's arrays. A program takes and returns all parts, laid end to end along the dimension named above; an argument that names none is the same for every part. Nothing has to cross between parts.
Inputs may be any that keep to these rules, and one draw needn't show every extreme that they name: block_counts[g] is the number of live blocks of group g: the first block_counts[g] of its 16 block slots hold encoder tokens, the rest are padding; in every draw some group has all 16 live.
All inputs are finite; a program needn't handle non-finite values.
Results may differ from the reference program's by a relative error of at most 0.023.
The reference program's roundings to bfloat16 on the way count: a program that leaves them out, or rounds other values in their place, can miss the bound.
Values may be sent and summed in bfloat16 or wider, within the bound.
A program may use at most 128 MiB of HBM per device.

```python
import math
import jax
import jax.numpy as jnp
from jax import lax

DE = 1024
HEADS = 32
HD = 128
D = 4096
BLOCK = 128
SEQ = 4096
GROUPS = 8
GROUP_BLOCKS = 16
ENC = 16384


def draw_enc_states(key, part):
    key = jax.random.fold_in(key, 5)
    first = jax.random.fold_in(key, 0)
    result = jnp.clip(jax.random.normal(first, (ENC, DE), jnp.float32), -6.0, 6.0)
    return result.astype(jnp.bfloat16)


def draw_block_counts(key, part):
    key = jax.random.fold_in(key, 3)
    first, second, third = jax.random.split(key, 3)
    one_draw = jax.random.randint(first, (GROUPS,), 1, GROUP_BLOCKS + 1)
    two_draw = jax.random.randint(second, (GROUPS,), 1, GROUP_BLOCKS + 1)
    counts_low = jnp.minimum(one_draw, two_draw)
    full_group = jax.random.randint(third, (), 0, GROUPS)
    return jnp.where(jnp.arange(GROUPS) == full_group, GROUP_BLOCKS, counts_low).astype(jnp.int32)


def levels(stream_key, extent, shards, least, top_value):
    def one(axis_at, shards_of):
        steps = jax.random.uniform(jax.random.fold_in(jax.random.fold_in(stream_key, 6), axis_at), (shards_of,), jnp.float32, least / len(shards), top_value / len(shards))
        return jnp.repeat(jnp.exp(steps), extent[axis_at] // shards_of).reshape((-1,) + (1,) * (len(extent) - axis_at - 1))

    loudness = one(*shards[0])
    for cut in shards[1:]:
        loudness = loudness * one(*cut)
    return loudness


def noise(rng, dims, scale, reach, pieces=(), kind=jnp.bfloat16):
    entries = jax.random.normal(rng, dims, jnp.float32) * scale
    if len(pieces) > 0:
        entries = levels(rng, dims, pieces, -0.22, 0.18) * entries
    return jnp.clip(entries, min=-reach, max=reach).astype(kind)


def setup_inputs(seed: int = 0, part: int = 0) -> dict:
    arg_keys = jax.random.split(jax.random.key(seed), 9)
    part_splits = jax.random.split(jax.random.fold_in(arg_keys[8], part), 9)
    return {
        "hidden_in": noise(part_splits[0], (SEQ, D), 1.0, 6.0, ((0, 8), (1, 16))),
        "norm_gain": jnp.clip(1.0 + 0.18 * jax.random.normal(arg_keys[1], (D,), jnp.float32), 0.099609375, 1.8984375).astype(jnp.bfloat16),
        "w_query": noise(arg_keys[2], (D, D), (D // 16) ** -0.5, 0.375, ((1, 16),)),
        "enc_states": draw_enc_states(jax.random.fold_in(jax.random.fold_in(arg_keys[8], part), 71), part),
        "w_key": noise(arg_keys[4], (DE, D), DE ** -0.5, 0.1875, ((1, 16),)),
        "w_value": noise(arg_keys[5], (DE, D), DE ** -0.5, 0.1875, ((1, 16),)),
        "w_out": noise(arg_keys[6], (D, D), HD ** -0.5, 0.5, ((0, 16),)),
        "block_counts": draw_block_counts(jax.random.fold_in(jax.random.fold_in(arg_keys[8], part), 71), part),
    }


def reference(hidden_in, norm_gain, w_query, enc_states, w_key, w_value, w_out, block_counts):
    row_values = hidden_in.astype(jnp.float32)
    mean_square = lax.optimization_barrier(jnp.mean(row_values * row_values, axis=1, keepdims=True))
    normed = (row_values * lax.rsqrt(mean_square + 1e-05) * norm_gain.astype(jnp.float32)).astype(jnp.bfloat16)
    queries = jnp.dot(normed, w_query, preferred_element_type=jnp.float32).astype(jnp.bfloat16)
    key_rows = jnp.dot(enc_states, w_key, preferred_element_type=jnp.float32).astype(jnp.bfloat16)
    value_rows = jnp.dot(enc_states, w_value, preferred_element_type=jnp.float32).astype(jnp.bfloat16)
    row_index = jnp.arange(enc_states.shape[0], dtype=jnp.int32)
    group_rows = BLOCK * GROUP_BLOCKS
    live_limit = block_counts[(row_index // group_rows).astype(jnp.int32)]
    is_live = row_index // BLOCK % GROUP_BLOCKS < live_limit
    seq_rows = queries.shape[0]
    query_heads = queries.reshape(seq_rows, HEADS, HD).transpose(1, 0, 2)
    key_heads = key_rows.reshape(-1, HEADS, HD).transpose(1, 0, 2)
    value_heads = value_rows.reshape(-1, HEADS, HD).transpose(1, 0, 2)
    scale = 1.0 / math.sqrt(HD)

    def one_head(operands):
        q_one, k_one, v_one = operands
        scores = jnp.dot(q_one, k_one.T, preferred_element_type=jnp.float32) * scale
        masked = jnp.where(is_live[None, :], scores, -1e+30)
        row_max = lax.optimization_barrier(jnp.max(masked, axis=1, keepdims=True))
        weights = jnp.where(is_live[None, :], jnp.exp(scores - row_max), 0.0)
        row_sum = lax.optimization_barrier(jnp.sum(weights, axis=1, keepdims=True))
        mixed_sum = jnp.dot(weights.astype(jnp.bfloat16), v_one, preferred_element_type=jnp.float32)
        return (mixed_sum / row_sum).astype(jnp.bfloat16)
    attended = lax.map(one_head, (query_heads, key_heads, value_heads))
    attended = attended.transpose(1, 0, 2).reshape(seq_rows, HEADS * HD)
    return jnp.dot(attended, w_out, preferred_element_type=jnp.float32).astype(jnp.bfloat16)
```

```python
import math

import jax
import jax.numpy as jnp
from jax import lax
from jax.experimental import pallas as pl
from jax.experimental.pallas import tpu as pltpu
from jax.sharding import PartitionSpec as P

HD = 128
X = 4
Y = 4
Z = 8
HEAD = X * Y
T = 256
CHUNKS = 2
F = 256
BLOCK = 128
SLOTS = 16
KEYS = BLOCK * SLOTS
DE = 1024
LOG2E = 1.4426950408889634
COEF = LOG2E / math.sqrt(HD)
NEG = -1e30
F32 = jnp.float32
BF16 = jnp.bfloat16
MESH = pl.DeviceIdType.MESH


def wrap(value, size):
    return lax.rem(value + 2 * size, size)


class Place:
    def __init__(self):
        self.dp = lax.axis_index("dp")
        self.z = lax.axis_index("span")
        self.head = lax.axis_index("head")
        self.x = lax.div(self.head, Y)
        self.y = lax.rem(self.head, Y)

    def slot(self, dx, dy):
        return wrap(self.x + dx, X) * Y + wrap(self.y + dy, Y)

    def at_xy(self, dx, dy):
        return (self.dp, self.z, self.slot(dx, dy))

    def at_z(self, dz):
        return (self.dp, wrap(self.z + dz, Z), self.head)


class Gather:
    REL = (0, -1, 1, 2)

    def __init__(self, place, buf, rows, send, recv):
        self.place, self.buf, self.rows, self.send, self.recv = place, buf, rows, send, recv
        self.started = []

    def shift(self, half, da, db):
        return (db, da) if half == 0 else (da, db)

    def part(self, half, da, db, quarter):
        base = half * (self.rows // 2)
        count = self.rows // 2
        if quarter is not None:
            count = self.rows // 4
            base = base + quarter * count
        return self.buf.at[self.place.slot(*self.shift(half, da, db)), pl.ds(base, count)]

    def copy(self, half, index, ref, to):
        return pltpu.make_async_remote_copy(
            src_ref=ref,
            dst_ref=ref,
            send_sem=self.send.at[half * 20 + index],
            recv_sem=self.recv.at[half * 20 + index],
            device_id=to,
            device_id_type=MESH,
        )

    def go(self, half, index, da, db, quarter, ta, tb):
        copy = self.copy(
            half,
            index,
            self.part(half, da, db, quarter),
            self.place.at_xy(*self.shift(half, ta, tb)),
        )
        copy.start()
        self.started.append(copy)

    def take(self, half, index, da, db, quarter):
        ref = self.part(half, da, db, quarter)
        self.copy(half, index, ref, self.place.at_xy(1, 0)).wait_recv()

    def line(self, half, which):
        base = 4 + 4 * which
        rel = self.REL[which]
        self.go(half, base, rel, 0, None, 0, 1)
        self.go(half, base + 1, rel, 0, None, 0, -1)

    def pass_on(self, half, which):
        base = 4 + 4 * which
        rel = self.REL[which]
        self.take(half, base, rel, -1, None)
        self.go(half, base + 2, rel, -1, 0, 0, 1)
        self.take(half, base + 1, rel, 1, None)
        self.go(half, base + 3, rel, 1, 1, 0, -1)

    def s0(self):
        for half in range(2):
            self.go(half, 0, 0, 0, None, 1, 0)
            self.go(half, 1, 0, 0, None, -1, 0)
        for half in range(2):
            self.line(half, 0)

    def s1(self):
        for half in range(2):
            self.take(half, 0, -1, 0, None)
            self.go(half, 2, -1, 0, 0, 1, 0)
            self.take(half, 1, 1, 0, None)
            self.go(half, 3, 1, 0, 1, -1, 0)
        for half in range(2):
            self.line(half, 1)
            self.line(half, 2)

    def s2(self):
        for half in range(2):
            self.pass_on(half, 0)

    def s3(self):
        for half in range(2):
            self.take(half, 2, 2, 0, 0)
            self.take(half, 3, 2, 0, 1)
            self.line(half, 3)

    def s4(self):
        for which in (1, 2):
            for half in range(2):
                self.pass_on(half, which)

    def s5(self):
        for half in range(2):
            self.pass_on(half, 3)

    def s6(self):
        for which in range(4):
            for half in range(2):
                base = 4 + 4 * which
                rel = self.REL[which]
                self.take(half, base + 2, rel, 2, 0)
                self.take(half, base + 3, rel, 2, 1)

    def finish(self):
        for copy in self.started:
            copy.wait_send()


class QueryRing:
    def __init__(self, place, buf, chunk, send, recv):
        self.place, self.buf, self.chunk, self.send, self.recv = place, buf, chunk, send, recv
        self.started = []

    def copy(self, way, step, dz):
        ref = self.buf.at[self.chunk, wrap(self.place.z + dz, Z)]
        if step == 3:
            ref = ref.at[pl.ds(way * HD, HD)]
        index = (self.chunk * 2 + way) * 4 + step
        return pltpu.make_async_remote_copy(
            src_ref=ref,
            dst_ref=ref,
            send_sem=self.send.at[index],
            recv_sem=self.recv.at[index],
            device_id=self.place.at_z(1 - 2 * way),
            device_id_type=MESH,
        )

    def go(self, step):
        for way in range(2):
            copy = self.copy(way, step, -step if way == 0 else step)
            copy.start()
            self.started.append(copy)

    def take(self, step):
        for way in range(2):
            self.copy(way, step, -1 - step if way == 0 else 1 + step).wait_recv()

    def finish(self):
        for copy in self.started:
            copy.wait_send()


def kernel(
    hidden_hbm, gain_ref, wq_hbm, enc_hbm, wk_hbm, wv_hbm, wo_hbm, count_ref, out_ref,
    hbuf, wq, wk, wv, wo, nbuf, ebuf, qbuf, kbuf, vbuf, sbuf, opart, spart,
    osend, orecv, ssend, srecv, attb,
    st1, rv1, st2, rv2, st3, rv3, st4, rv4, sums, msend, mrecv,
    local_sem, ms_ss, ms_rs, ag_ss, ag_rs, q_ss, q_rs, o_ss, o_rs, x_ss, x_rs,
):
    place = Place()
    me = place.head
    z = place.z

    local = [
        pltpu.make_async_copy(source, target, local_sem.at[index])
        for index, (source, target) in enumerate(
            (
                (hidden_hbm, hbuf),
                (enc_hbm, ebuf.at[me]),
                (wq_hbm, wq),
                (wk_hbm, wk),
                (wv_hbm, wv),
                (wo_hbm, wo),
            )
        )
    ]
    for copy in local:
        copy.start()

    barrier = pltpu.get_barrier_semaphore()
    partners = [place.at_xy(d, 0) for d in (1, 2, 3)]
    partners += [place.at_xy(0, d) for d in (1, 2, 3)]
    partners += [place.at_z(1), place.at_z(-1)]
    for partner in partners:
        pl.semaphore_signal(barrier, inc=1, device_id=partner, device_id_type=MESH)

    for chunk in range(CHUNKS):
        orecv[chunk, 0, 0, HD:] = jnp.zeros((HD, T), BF16)
        orecv[chunk, 1, 0, :HD] = jnp.zeros((HD, T), BF16)

    local[0].wait()
    hid = hbuf[...].astype(F32)
    squares = hid * hid
    squares = squares[:, :128] + squares[:, 128:]
    total = jnp.sum(squares.T, axis=0, keepdims=True)
    pl.semaphore_wait(barrier, len(partners))
    ms_started = []

    def ms_copy(stage, d):
        index = stage * 3 + d - 1
        to = place.at_xy(0, d) if stage == 0 else place.at_xy(d, 0)
        return pltpu.make_async_remote_copy(
            src_ref=msend.at[stage],
            dst_ref=mrecv.at[stage, d - 1],
            send_sem=ms_ss.at[index],
            recv_sem=ms_rs.at[index],
            device_id=to,
            device_id_type=MESH,
        )

    def ms_send(stage, value):
        msend[stage] = jnp.broadcast_to(value, (8, CHUNKS * T))
        for d in (1, 2, 3):
            copy = ms_copy(stage, d)
            copy.start()
            ms_started.append(copy)

    def ms_take(stage, value):
        for d in (1, 2, 3):
            ms_copy(stage, d).wait_recv()
        for d in (1, 2, 3):
            value = value + mrecv[stage, d - 1, 0:1, :]
        return value

    gather_e = Gather(place, ebuf, BLOCK, ag_ss.at[0], ag_rs.at[0])
    gather_a = Gather(place, nbuf.at[0], T, ag_ss.at[1], ag_rs.at[1])
    gather_b = Gather(place, nbuf.at[1], T, ag_ss.at[2], ag_rs.at[2])
    ring_a = QueryRing(place, qbuf, 0, q_ss, q_rs)
    ring_b = QueryRing(place, qbuf, 1, q_ss, q_rs)

    ms_send(0, total)
    local[1].wait()
    gather_e.s0()
    total = ms_take(0, total)
    ms_send(1, total)
    total = ms_take(1, total)
    inverse = lax.rsqrt(total * (1.0 / (HEAD * F)) + 1e-05)
    column = jnp.broadcast_to(inverse, (128, CHUNKS * T)).T
    gain = gain_ref[...].astype(F32)
    for side in range(2):
        cols = pl.ds(side * 128, 128)
        normed = hbuf[:, cols].astype(F32) * column * gain[:, side * 128 : side * 128 + 128]
        normed = normed.astype(BF16)
        for chunk in range(CHUNKS):
            nbuf[chunk, pl.ds(me, 1), :, cols] = normed[chunk * T : (chunk + 1) * T][None]

    def project(chunk):
        acc = jnp.zeros((T, F), F32)
        for source in range(HEAD):
            acc = acc + jnp.dot(
                nbuf[chunk, source], wq[source * F : (source + 1) * F], preferred_element_type=F32
            )
        qbuf[chunk, pl.ds(z, 1)] = acc.T.astype(BF16)[None]

    live_blocks = count_ref[z]

    def live_mask(block, shape):
        return (jnp.zeros(shape, jnp.int32) + block) < live_blocks

    def encode(part):
        rows = ebuf[4 * part : 4 * part + 4].reshape(4 * BLOCK, DE)
        keys = jnp.dot(rows, wk[...], preferred_element_type=F32)
        values = jnp.dot(rows, wv[...], preferred_element_type=F32)
        for inner in range(4):
            block = 4 * part + inner
            live = live_mask(block, (BLOCK, HD))
            span = slice(inner * BLOCK, (inner + 1) * BLOCK)
            for head in range(2):
                cols = slice(head * HD, (head + 1) * HD)
                key_block = keys[span, cols]
                if block > 0:
                    key_block = jnp.where(live, key_block, kbuf[head, :BLOCK].astype(F32))
                kbuf[head, block * BLOCK : (block + 1) * BLOCK] = key_block.astype(BF16)
                value_block = jnp.where(live, values[span, cols], 0.0)
                vbuf[cols, block * BLOCK : (block + 1) * BLOCK] = value_block.T.astype(BF16)

    gather_a.s0()
    gather_b.s0()
    gather_a.s1()
    gather_a.s2()
    gather_a.s3()
    gather_b.s1()
    gather_a.s4()
    gather_a.s5()
    gather_b.s2()
    gather_b.s3()
    gather_a.s6()
    local[2].wait()
    project(0)
    ring_a.go(0)
    gather_b.s4()
    gather_b.s5()
    gather_e.s1()
    ring_a.take(0)
    ring_a.go(1)
    gather_e.s2()
    gather_e.s3()
    gather_b.s6()
    project(1)
    ring_b.go(0)
    ring_a.take(1)
    ring_a.go(2)
    gather_e.s4()
    ring_a.take(2)
    ring_a.go(3)
    ring_b.take(0)
    ring_b.go(1)
    gather_e.s5()
    ring_b.take(1)
    ring_b.go(2)
    gather_e.s6()
    ring_b.take(2)
    ring_b.go(3)
    local[3].wait()
    local[4].wait()
    for part in range(4):
        encode(part)
    ring_a.take(3)
    ring_b.take(3)
    local[5].wait()

    live_row = [jnp.where(live_mask(block, (1, T)), 1.0, 0.0) for block in range(SLOTS)]

    def attend(chunk, plane):
        for head in range(2):
            query = qbuf[chunk, pl.ds(plane, 1), head * HD : (head + 1) * HD, :][0]
            best = None
            for piece in range(KEYS // 256):
                span = slice(piece * 256, (piece + 1) * 256)
                scores = jnp.dot(kbuf[head, span], query, preferred_element_type=F32)
                sbuf[head, span] = scores
                top = jnp.max(scores.reshape(32, 8, T), axis=0)
                best = top if best is None else jnp.maximum(best, top)
            best = jnp.max(best, axis=0, keepdims=True) * COEF
            acc = jnp.zeros((HD, T), F32)
            total = jnp.zeros((8, T), F32)
            for piece in range(KEYS // 256):
                span = slice(piece * 256, (piece + 1) * 256)
                weights = jnp.exp2(sbuf[head, span] * COEF - best)
                for inner in range(2):
                    block_sum = jnp.sum(
                        weights[inner * BLOCK : (inner + 1) * BLOCK].reshape(16, 8, T), axis=0
                    )
                    total = total + block_sum * live_row[piece * 2 + inner]
                acc = acc + jnp.dot(
                    vbuf[head * HD : (head + 1) * HD, span],
                    weights.astype(BF16),
                    preferred_element_type=F32,
                )
            opart[head * HD : (head + 1) * HD] = acc
            spart[2 * head : 2 * head + 1] = best
            spart[2 * head + 1 : 2 * head + 2] = jnp.sum(total, axis=0, keepdims=True)

    def merge(chunk, way, step):
        for head in range(2):
            rows = slice(head * HD, (head + 1) * HD)
            best_a = spart[2 * head : 2 * head + 1]
            best_b = srecv[chunk, way, step, 2 * head : 2 * head + 1, :]
            sum_a = spart[2 * head + 1 : 2 * head + 2]
            sum_b = srecv[chunk, way, step, 2 * head + 1 : 2 * head + 2, :]
            best = jnp.maximum(best_a, best_b)
            scale_a = jnp.exp2(best_a - best)
            scale_b = jnp.exp2(best_b - best)
            spart[2 * head : 2 * head + 1] = best
            spart[2 * head + 1 : 2 * head + 2] = sum_a * scale_a + sum_b * scale_b
            opart[rows] = (
                opart[rows] * scale_a + orecv[chunk, way, step, rows, :].astype(F32) * scale_b
            )

    def o_copies(chunk, way, step, first):
        index = ((chunk * 2 + way) * 4 + step) * 2
        to = (place.dp, wrap(z + 1 - 2 * way, Z), place.head)
        source, target = osend.at[chunk, way, step], orecv.at[chunk, way, step]
        if first:
            source, target = source.at[pl.ds(way * HD, HD)], target.at[pl.ds(way * HD, HD)]
        return [
            pltpu.make_async_remote_copy(
                src_ref=src,
                dst_ref=dst,
                send_sem=o_ss.at[index + which],
                recv_sem=o_rs.at[index + which],
                device_id=to,
                device_id_type=MESH,
            )
            for which, (src, dst) in enumerate(
                ((source, target), (ssend.at[chunk, way, step], srecv.at[chunk, way, step]))
            )
        ]

    def out_axes(half, da, db):
        return (da, db) if half == 0 else (db, da)

    def out_copy(chunk, half, way, step):
        send, recv = ((st1, rv1), (st2, rv2), (st3, rv3), (st4, rv4))[step]
        off = 1 - 2 * way
        to = place.at_xy(*out_axes(half, off, 0) if step < 2 else out_axes(half, 0, off))
        index = ((chunk * 2 + half) * 2 + way) * 4 + step
        return pltpu.make_async_remote_copy(
            src_ref=send.at[chunk, half, way],
            dst_ref=recv.at[chunk, half, way],
            send_sem=x_ss.at[index],
            recv_sem=x_rs.at[index],
            device_id=to,
            device_id_type=MESH,
        )

    def out_part(chunk, half, da, db):
        slot = place.slot(*out_axes(half, da, db))
        return jnp.dot(
            attb[chunk, half * 128 : (half + 1) * 128],
            wo[:, pl.ds(pl.multiple_of(slot * F, F), F)],
            preferred_element_type=F32,
        )

    def out_take(chunk, step):
        for half in range(2):
            for way in range(2):
                out_copy(chunk, half, way, step).wait_recv()

    def out_1(chunk):
        for half in range(2):
            for db in range(4):
                part = out_part(chunk, half, 2, db).astype(BF16)
                st1[chunk, half, 0, db] = part[:64]
                st1[chunk, half, 1, db] = part[64:]
            for way in range(2):
                out_copy(chunk, half, way, 0).start()

    def out_2(chunk):
        out_take(chunk, 0)
        for half in range(2):
            for way in range(2):
                for db in range(4):
                    part = out_part(chunk, half, 1 - 2 * way, db)
                    other = rv1[chunk, half, way, db].astype(F32)
                    if way == 0:
                        st2[chunk, half, way, db, :64] = (part[:64] + other).astype(BF16)
                        st2[chunk, half, way, db, 64:] = part[64:].astype(BF16)
                    else:
                        st2[chunk, half, way, db, :64] = part[:64].astype(BF16)
                        st2[chunk, half, way, db, 64:] = (part[64:] + other).astype(BF16)
                out_copy(chunk, half, way, 1).start()

    def out_3(chunk):
        out_take(chunk, 1)
        for half in range(2):
            for db in (2, 1, 3, 0):
                part = out_part(chunk, half, 0, db)
                part = part + rv2[chunk, half, 0, db].astype(F32)
                part = part + rv2[chunk, half, 1, db].astype(F32)
                if db == 2:
                    st3[chunk, half, 0] = part[:64].astype(BF16)
                    st3[chunk, half, 1] = part[64:].astype(BF16)
                    for way in range(2):
                        out_copy(chunk, half, way, 2).start()
                else:
                    sums[half, (1, 3, 0).index(db)] = part

    def out_4(chunk):
        out_take(chunk, 2)
        for half in range(2):
            part = sums[half, 0]
            st4[chunk, half, 0, :64] = (part[:64] + rv3[chunk, half, 0].astype(F32)).astype(BF16)
            st4[chunk, half, 0, 64:] = part[64:].astype(BF16)
            out_copy(chunk, half, 0, 3).start()
            part = sums[half, 1]
            st4[chunk, half, 1, :64] = part[:64].astype(BF16)
            st4[chunk, half, 1, 64:] = (part[64:] + rv3[chunk, half, 1].astype(F32)).astype(BF16)
            out_copy(chunk, half, 1, 3).start()

    def out_5(chunk):
        out_take(chunk, 3)
        for half in range(2):
            part = sums[half, 2] + rv4[chunk, half, 0].astype(F32)
            part = part + rv4[chunk, half, 1].astype(F32)
            start = chunk * T + half * 128
            out_ref[start : start + 128] = part.astype(BF16)

    def one_block(n, carry):
        chunk = lax.div(n, 8)
        i = lax.rem(n, 8)
        step = lax.div(i + 1, 2)
        way = lax.rem(i + 1, 2)
        plane = wrap(z + (1 - 2 * way) * (4 - step), Z)
        attend(chunk, plane)

        @pl.when(i == 0)
        def _():
            neutral_best = jnp.full((1, T), NEG, F32)
            neutral_sum = jnp.zeros((1, T), F32)
            for w in range(2):
                rows = slice(w * HD, (w + 1) * HD)
                osend[chunk, w, 0, rows] = opart[rows].astype(BF16)
                ssend[chunk, w, 0, 2 * w : 2 * w + 2] = spart[2 * w : 2 * w + 2]
                o = 1 - w
                ssend[chunk, w, 0, 2 * o : 2 * o + 1] = neutral_best
                ssend[chunk, w, 0, 2 * o + 1 : 2 * o + 2] = neutral_sum
                for copy in o_copies(chunk, w, 0, True):
                    copy.start()

        @pl.when(jnp.logical_and(i > 0, i < 7))
        def _():
            @pl.when(step == 1)
            def _():
                first_take(chunk, way)

            @pl.when(step > 1)
            def _():
                for copy in o_copies(chunk, way, step - 1, False):
                    copy.wait_recv()

            merge(chunk, way, step - 1)
            osend[chunk, way, step] = opart[...].astype(BF16)
            ssend[chunk, way, step] = spart[...]
            for copy in o_copies(chunk, way, step, False):
                copy.start()

        @pl.when(i == 7)
        def _():
            for w in range(2):
                for copy in o_copies(chunk, w, 3, False):
                    copy.wait_recv()
                merge(chunk, w, 3)
            for head in range(2):
                rows = slice(head * HD, (head + 1) * HD)
                done = opart[rows] / spart[2 * head + 1 : 2 * head + 2]
                attb[chunk, :, rows] = done.T.astype(BF16)

        for at, work in ((8, out_1), (10, out_2), (12, out_3), (14, out_4)):
            pl.when(n == at)(lambda work=work: work(0))
        return carry

    def first_take(chunk, way):
        for w in range(2):
            @pl.when(way == w)
            def _():
                for copy in o_copies(chunk, w, 0, True):
                    copy.wait_recv()

    spart[...] = jnp.zeros((8, T), F32)
    lax.fori_loop(0, 8 * CHUNKS, one_block, 0)
    out_5(0)
    out_1(1)
    out_2(1)
    out_3(1)
    out_4(1)
    out_5(1)

    for copy in ms_started:
        copy.wait_send()
    for gather in (gather_e, gather_a, gather_b, ring_a, ring_b):
        gather.finish()
    for chunk in range(CHUNKS):
        for way in range(2):
            for step in range(4):
                for copy in o_copies(chunk, way, step, step == 0):
                    copy.wait_send()
                for half in range(2):
                    out_copy(chunk, half, way, step).wait_send()


def per_device(hidden_in, norm_gain, w_query, enc_states, w_key, w_value, w_out, block_counts):
    any_spec = pl.BlockSpec(memory_space=pl.ANY)
    vmem = pltpu.VMEM
    dma = pltpu.SemaphoreType.DMA
    scratch = [
        vmem((CHUNKS * T, F), BF16),
        vmem((HEAD * F, F), BF16),
        vmem((DE, F), BF16),
        vmem((DE, F), BF16),
        vmem((F, HEAD * F), BF16),
        vmem((CHUNKS, HEAD, T, F), BF16),
        vmem((HEAD, BLOCK, DE), BF16),
        vmem((CHUNKS, Z, F, T), BF16),
        vmem((2, KEYS, HD), BF16),
        vmem((F, KEYS), BF16),
        vmem((2, KEYS, T), F32),
        vmem((F, T), F32),
        vmem((8, T), F32),
        vmem((CHUNKS, 2, 4, F, T), BF16),
        vmem((CHUNKS, 2, 4, F, T), BF16),
        vmem((CHUNKS, 2, 4, 8, T), F32),
        vmem((CHUNKS, 2, 4, 8, T), F32),
        vmem((CHUNKS, T, F), BF16),
        vmem((CHUNKS, 2, 2, 4, 64, F), BF16),
        vmem((CHUNKS, 2, 2, 4, 64, F), BF16),
        vmem((CHUNKS, 2, 2, 4, 128, F), BF16),
        vmem((CHUNKS, 2, 2, 4, 128, F), BF16),
        vmem((CHUNKS, 2, 2, 64, F), BF16),
        vmem((CHUNKS, 2, 2, 64, F), BF16),
        vmem((CHUNKS, 2, 2, 128, F), BF16),
        vmem((CHUNKS, 2, 2, 128, F), BF16),
        vmem((2, 3, 128, F), F32),
        vmem((2, 8, CHUNKS * T), F32),
        vmem((2, 3, 8, CHUNKS * T), F32),
        dma((6,)),
        dma((6,)),
        dma((6,)),
        dma((3, 40)),
        dma((3, 40)),
        dma((CHUNKS * 8,)),
        dma((CHUNKS * 8,)),
        dma((CHUNKS * 16,)),
        dma((CHUNKS * 16,)),
        dma((CHUNKS * 16,)),
        dma((CHUNKS * 16,)),
    ]
    return pl.pallas_call(
        kernel,
        out_shape=jax.ShapeDtypeStruct((CHUNKS * T, F), BF16),
        in_specs=[
            any_spec,
            pl.BlockSpec(memory_space=pltpu.VMEM),
            any_spec,
            any_spec,
            any_spec,
            any_spec,
            any_spec,
            pl.BlockSpec(memory_space=pltpu.SMEM),
        ],
        out_specs=pl.BlockSpec(memory_space=pltpu.VMEM),
        scratch_shapes=scratch,
        compiler_params=pltpu.CompilerParams(
            collective_id=0, has_side_effects=True, vmem_limit_bytes=60 * 1024 * 1024
        ),
        cost_estimate=pl.CostEstimate(
            flops=13_000_000_000, bytes_accessed=8_000_000, transcendentals=17_000_000
        ),
    )(
        hidden_in, norm_gain.reshape(1, F), w_query, enc_states, w_key, w_value, w_out, block_counts
    )


def solution(mesh):
    placed = (
        P(("dp", "span"), "head"),
        P("head"),
        P(None, "head"),
        P(("dp", "span", "head"), None),
        P(None, "head"),
        P(None, "head"),
        P("head", None),
        P("dp"),
    )
    return jax.shard_map(
        per_device, mesh=mesh, in_specs=placed, out_specs=P(("dp", "span"), "head"), check_vma=False
    )
```

```python
import math

import jax
import jax.numpy as jnp
from jax import lax
from jax.experimental import pallas as pl
from jax.experimental.pallas import tpu as pltpu
from jax.sharding import PartitionSpec as P

HD = 128
X = 4
Y = 4
Z = 8
HEAD = X * Y
T = 256
CHUNKS = 2
F = 256
BLOCK = 128
SLOTS = 16
KEYS = BLOCK * SLOTS
TILE = 256
DE = 1024
LOG2E = 1.4426950408889634
COEF = LOG2E / math.sqrt(HD)
NEG = -1e30
F32 = jnp.float32
BF16 = jnp.bfloat16
MESH = pl.DeviceIdType.MESH


def div(value, by):
    return value // by if isinstance(value, int) else lax.div(value, by)


def rem(value, by):
    return value % by if isinstance(value, int) else lax.rem(value, by)


def wrap(value, size):
    return rem(value + 2 * size, size)


class Place:
    def __init__(self):
        self.dp = lax.axis_index("dp")
        self.z = lax.axis_index("span")
        self.head = lax.axis_index("head")
        self.x = div(self.head, Y)
        self.y = rem(self.head, Y)

    def slot(self, dx, dy):
        return wrap(self.x + dx, X) * Y + wrap(self.y + dy, Y)

    def at_xy(self, dx, dy):
        return (self.dp, self.z, self.slot(dx, dy))

    def at_z(self, dz):
        return (self.dp, wrap(self.z + dz, Z), self.head)


class Gather:
    REL = (0, -1, 1, 2)

    def __init__(self, place, buf, rows, send, recv):
        self.place, self.buf, self.rows, self.send, self.recv = place, buf, rows, send, recv
        self.started = []

    def shift(self, half, da, db):
        return (db, da) if half == 0 else (da, db)

    def part(self, half, da, db, quarter):
        base = half * (self.rows // 2)
        count = self.rows // 2
        if quarter is not None:
            count = self.rows // 4
            base = base + quarter * count
        return self.buf.at[self.place.slot(*self.shift(half, da, db)), pl.ds(base, count)]

    def copy(self, half, index, ref, to):
        return pltpu.make_async_remote_copy(
            src_ref=ref,
            dst_ref=ref,
            send_sem=self.send.at[half * 20 + index],
            recv_sem=self.recv.at[half * 20 + index],
            device_id=to,
            device_id_type=MESH,
        )

    def sent(self, half, index, da, db, quarter, ta, tb):
        ref = self.part(half, da, db, quarter)
        return self.copy(half, index, ref, self.place.at_xy(*self.shift(half, ta, tb)))

    def go(self, *what):
        self.sent(*what).start()
        self.started.append(what)

    def take(self, half, index, da, db, quarter):
        ref = self.part(half, da, db, quarter)
        self.copy(half, index, ref, self.place.at_xy(1, 0)).wait_recv()

    def line(self, half, which):
        base = 4 + 4 * which
        rel = self.REL[which]
        self.go(half, base, rel, 0, None, 0, 1)
        self.go(half, base + 1, rel, 0, None, 0, -1)

    def pass_on(self, half, which):
        base = 4 + 4 * which
        rel = self.REL[which]
        self.take(half, base, rel, -1, None)
        self.go(half, base + 2, rel, -1, 0, 0, 1)
        self.take(half, base + 1, rel, 1, None)
        self.go(half, base + 3, rel, 1, 1, 0, -1)

    def s0(self):
        for half in range(2):
            self.go(half, 0, 0, 0, None, 1, 0)
            self.go(half, 1, 0, 0, None, -1, 0)
        for half in range(2):
            self.line(half, 0)

    def s1(self):
        for half in range(2):
            self.take(half, 0, -1, 0, None)
            self.go(half, 2, -1, 0, 0, 1, 0)
            self.take(half, 1, 1, 0, None)
            self.go(half, 3, 1, 0, 1, -1, 0)
        for half in range(2):
            self.line(half, 1)
            self.line(half, 2)

    def s2(self):
        for half in range(2):
            self.pass_on(half, 0)

    def s3(self):
        for half in range(2):
            self.take(half, 2, 2, 0, 0)
            self.take(half, 3, 2, 0, 1)
            self.line(half, 3)

    def s4(self):
        for which in (1, 2):
            for half in range(2):
                self.pass_on(half, which)

    def s5(self):
        for half in range(2):
            self.pass_on(half, 3)

    def s6(self):
        for which in range(4):
            for half in range(2):
                base = 4 + 4 * which
                rel = self.REL[which]
                self.take(half, base + 2, rel, 2, 0)
                self.take(half, base + 3, rel, 2, 1)

    def finish(self):
        for what in self.started:
            self.sent(*what).wait_send()


class QueryRing:
    def __init__(self, place, buf, chunk, send, recv):
        self.place, self.buf, self.chunk, self.send, self.recv = place, buf, chunk, send, recv
        self.started = []

    def copy(self, way, step, head, dz):
        ref = self.buf.at[self.chunk, wrap(self.place.z + dz, Z), pl.ds(head * HD, HD)]
        index = ((self.chunk * 2 + way) * 4 + step) * 2 + head
        return pltpu.make_async_remote_copy(
            src_ref=ref,
            dst_ref=ref,
            send_sem=self.send.at[index],
            recv_sem=self.recv.at[index],
            device_id=self.place.at_z(1 - 2 * way),
            device_id_type=MESH,
        )

    def go(self, way, step, head):
        if step == 3 and head != way:
            return
        what = (way, step, head, -step if way == 0 else step)
        self.copy(*what).start()
        self.started.append(what)

    def begin(self):
        for head in range(2):
            for way in range(2):
                self.go(way, 0, head)

    def hop(self, step):
        for head in range(2):
            for way in range(2):
                if step == 3 and head != way:
                    continue
                self.copy(way, step, head, -1 - step if way == 0 else 1 + step).wait_recv()
                if step < 3:
                    self.go(way, step + 1, head)

    def finish(self):
        for what in self.started:
            self.copy(*what).wait_send()


def kernel(
    hidden_hbm, gain_ref, wq_hbm, enc_hbm, wk_hbm, wv_hbm, wo_hbm, count_ref, out_ref,
    wq, wk, wv, wo, nbuf, ebuf, qbuf, kbuf, vbuf, score_0, score_1, best_0, best_1, blocks_o, blocks_s, live_buf,

    osend, orecv, attb,
    st1, rv1, st2, rv2, st3, rv3, st4, rv4, parts, gains,
    local_sem, ms_ss, ms_rs, ag_ss, ag_rs, q_ss, q_rs, o_ss, o_rs, x_ss, x_rs,
):
    place = Place()
    me = place.head
    z = place.z

    local = [
        pltpu.make_async_copy(source, target, local_sem.at[index])
        for index, (source, target) in enumerate(
            (
                (hidden_hbm.at[pl.ds(0, T)], nbuf.at[0, me]),
                (hidden_hbm.at[pl.ds(T, T)], nbuf.at[1, me]),
                (enc_hbm, ebuf.at[me]),
                (wq_hbm, wq),
                (wk_hbm, wk),
                (wv_hbm, wv),
                (wo_hbm, wo),
            )
        )
    ]
    for copy in local:
        copy.start()

    barrier = pltpu.get_barrier_semaphore()
    partners = [place.at_xy(d, 0) for d in (1, 2, 3)]
    partners += [place.at_xy(0, d) for d in (1, 2, 3)]
    partners += [place.at_z(1), place.at_z(-1)]
    for partner in partners:
        pl.semaphore_signal(barrier, inc=1, device_id=partner, device_id_type=MESH)

    gains[pl.ds(me, 1)] = jnp.broadcast_to(gain_ref[...].astype(F32).reshape(1, 1, F), (1, 8, F))

    def gain_copy(stage, d, behind=0):
        if stage == 0:
            ref, to = gains.at[place.slot(0, -behind)], place.at_xy(0, d)
        else:
            ref, to = gains.at[pl.ds(wrap(place.x - behind, X) * Y, Y)], place.at_xy(d, 0)
        return pltpu.make_async_remote_copy(
            src_ref=ref,
            dst_ref=ref,
            send_sem=ms_ss.at[stage * 3 + d - 1],
            recv_sem=ms_rs.at[stage * 3 + d - 1],
            device_id=to,
            device_id_type=MESH,
        )

    def gain_go(stage):
        for d in (1, 2, 3):
            gain_copy(stage, d).start()

    def gain_take(stage):
        for d in (1, 2, 3):
            gain_copy(stage, d, d).wait_recv()

    gather_e = Gather(place, ebuf, BLOCK, ag_ss.at[0], ag_rs.at[0])
    gather_a = Gather(place, nbuf.at[0], T, ag_ss.at[1], ag_rs.at[1])
    gather_b = Gather(place, nbuf.at[1], T, ag_ss.at[2], ag_rs.at[2])
    ring_a = QueryRing(place, qbuf, 0, q_ss, q_rs)
    ring_b = QueryRing(place, qbuf, 1, q_ss, q_rs)

    def project(chunk):
        squares = jnp.zeros((T, F), F32)
        for source in range(HEAD):
            rows = nbuf[chunk, source].astype(F32)
            squares = squares + rows * rows
        mean = jnp.sum(squares, axis=1, keepdims=True) * (1.0 / (HEAD * F))
        inverse = lax.rsqrt(mean + 1e-05)
        acc = jnp.zeros((T, F), F32)
        for source in range(HEAD):
            rows = nbuf[chunk, source].astype(F32) * inverse * gains[source, 0:1, :]
            acc = acc + jnp.dot(
                rows.astype(BF16), wq[source * F : (source + 1) * F], preferred_element_type=F32
            )
        qbuf[chunk, pl.ds(z, 1)] = acc.T.astype(BF16)[None]

    live_blocks = count_ref[z]

    def encode():
        for part in range(4):
            rows = ebuf[4 * part : 4 * part + 4].reshape(4 * BLOCK, DE)
            keys = jnp.dot(rows, wk[...], preferred_element_type=F32)
            values = jnp.dot(rows, wv[...], preferred_element_type=F32)
            slot = lax.broadcasted_iota(jnp.int32, (4 * BLOCK, HD), 0) // BLOCK + 4 * part
            live = slot < live_blocks
            span = pl.ds(part * 4 * BLOCK, 4 * BLOCK)
            for head in range(2):
                cols = slice(head * HD, (head + 1) * HD)
                key_block = keys[:, cols]
                lead = key_block[:BLOCK] if part == 0 else kbuf[head, :BLOCK].astype(F32)
                lead = jnp.concatenate([lead] * 4, axis=0)
                kbuf[head, span] = jnp.where(live, key_block, lead).astype(BF16)
                vbuf[cols, span] = jnp.where(live, values[:, cols], 0.0).T.astype(BF16)

    blocks_s[...] = jnp.zeros((CHUNKS * Z, 8, T), F32)
    for slot in range(SLOTS):
        alive = (jnp.zeros((8, T), jnp.int32) + slot) < live_blocks
        live_buf[slot] = jnp.where(alive, 1.0, 0.0)

    pl.semaphore_wait(barrier, len(partners))
    local[0].wait()
    gather_a.s0()
    local[1].wait()
    gather_b.s0()
    gain_go(0)
    gather_a.s1()
    gather_a.s2()
    gain_take(0)
    gain_go(1)
    gather_a.s3()
    gather_b.s1()
    gather_a.s4()
    gather_a.s5()
    gather_b.s2()
    gather_b.s3()
    gather_a.s6()
    gain_take(1)
    local[3].wait()
    project(0)
    ring_a.begin()
    gather_b.s4()
    gather_b.s5()
    local[2].wait()
    gather_e.s0()
    ring_a.hop(0)
    gather_b.s6()
    project(1)
    ring_b.begin()
    ring_a.hop(1)
    gather_e.s1()
    ring_b.hop(0)
    gather_e.s2()
    gather_e.s3()
    ring_a.hop(2)
    ring_b.hop(1)
    gather_e.s4()
    ring_a.hop(3)
    ring_b.hop(2)
    gather_e.s5()
    ring_b.hop(3)
    gather_e.s6()
    local[4].wait()
    local[5].wait()
    encode()
    local[6].wait()

    score_buf = (score_0, score_1)
    best_buf = (best_0, best_1)

    def sides(i):
        step = div(i + 1, 2)
        way = rem(i + 1, 2)
        return step, way, wrap(z + (1 - 2 * way) * (4 - step), Z)

    def phase(soft, soft_head, block, head):
        if block is not None:
            query = qbuf[div(block, 8), sides(rem(block, 8))[2], pl.ds(head * HD, HD), :]
            top = None
        if soft is not None:
            best = best_buf[soft_head][0:1, :]
            acc = jnp.zeros((HD, T), F32)
            total = jnp.zeros((8, T), F32)
        for tile in range(KEYS // TILE):
            span = slice(tile * TILE, (tile + 1) * TILE)
            if block is not None:
                scores = jnp.dot(kbuf[head, span], query, preferred_element_type=F32)
                score_buf[head][span] = scores
                peak = jnp.max(scores.reshape(TILE // 8, 8, T), axis=0)
                top = peak if top is None else jnp.maximum(top, peak)
            if soft is not None:
                weights = jnp.exp2(score_buf[soft_head][span] * COEF - best)
                for inner in range(TILE // BLOCK):
                    rows = weights[inner * BLOCK : (inner + 1) * BLOCK]
                    rows = jnp.sum(rows.reshape(BLOCK // 8, 8, T), axis=0)
                    total = total + rows * live_buf[tile * (TILE // BLOCK) + inner]
                acc = acc + jnp.dot(
                    vbuf[soft_head * HD : (soft_head + 1) * HD, span],
                    weights.astype(BF16),
                    preferred_element_type=F32,
                )
        if block is not None:
            top = jnp.max(top, axis=0, keepdims=True) * COEF
            best_buf[head][...] = jnp.broadcast_to(top, (8, T))
        if soft is not None:
            blocks_o[soft, pl.ds(soft_head * HD, HD)] = acc
            blocks_s[soft, pl.ds(2 * soft_head, 1)] = best
            blocks_s[soft, pl.ds(2 * soft_head + 1, 1)] = jnp.sum(total, axis=0, keepdims=True)

    def split3(value):
        high = value.astype(BF16).astype(F32)
        middle = (value - high).astype(BF16).astype(F32)
        return [high, middle, value - high - middle]

    def o_copy(chunk, way, step, head):
        index = ((chunk * 2 + way) * 4 + step) * 2 + head
        return pltpu.make_async_remote_copy(
            src_ref=osend.at[chunk, way, step, head],
            dst_ref=orecv.at[chunk, way, step, head],
            send_sem=o_ss.at[index],
            recv_sem=o_rs.at[index],
            device_id=(place.dp, wrap(z + 1 - 2 * way, Z), place.head),
            device_id_type=MESH,
        )

    def send_part(chunk, block, way, step, head):
        osend[chunk, way, step, head, :HD] = blocks_o[block, pl.ds(head * HD, HD), :].astype(BF16)
        rows = split3(blocks_s[block, pl.ds(2 * head, 1), :])
        rows += split3(blocks_s[block, pl.ds(2 * head + 1, 1), :])
        rows = jnp.concatenate(rows + [jnp.zeros((10, T), F32)], axis=0)
        osend[chunk, way, step, head, HD:] = rows.astype(BF16)
        o_copy(chunk, way, step, head).start()

    def merge_part(chunk, block, way, step, head):
        o_copy(chunk, way, step, head).wait_recv()
        rows = pl.ds(head * HD, HD)
        best_row = pl.ds(2 * head, 1)
        sum_row = pl.ds(2 * head + 1, 1)
        stats = orecv[chunk, way, step, head, HD:, :].astype(F32)
        best_a = blocks_s[block, best_row, :]
        best_b = stats[0:1] + stats[1:2] + stats[2:3]
        sum_b = stats[3:4] + stats[4:5] + stats[5:6]
        best = jnp.maximum(best_a, best_b)
        scale_a = jnp.exp2(best_a - best)
        scale_b = jnp.exp2(best_b - best)
        blocks_s[block, best_row] = best
        blocks_s[block, sum_row] = blocks_s[block, sum_row, :] * scale_a + sum_b * scale_b
        blocks_o[block, rows] = (
            blocks_o[block, rows, :] * scale_a
            + orecv[chunk, way, step, head, :HD, :].astype(F32) * scale_b
        )

    def out_axes(half, da, db):
        return (da, db) if half == 0 else (db, da)

    def out_copy(chunk, half, way, step, db=0):
        send, recv = ((st1, rv1), (st2, rv2), (st3, rv3), (st4, rv4))[step]
        off = 1 - 2 * way
        to = place.at_xy(*out_axes(half, off, 0) if step < 2 else out_axes(half, 0, off))
        index = ((chunk * 2 + half) * 2 + way) * 10 + (step * 4 + db if step < 2 else 6 + step)
        source, target = send.at[chunk, half, way], recv.at[chunk, half, way]
        if step < 2:
            source, target = source.at[db], target.at[db]
        return pltpu.make_async_remote_copy(
            src_ref=source,
            dst_ref=target,
            send_sem=x_ss.at[index],
            recv_sem=x_rs.at[index],
            device_id=to,
            device_id_type=MESH,
        )

    def out_part(chunk, half, da, db):
        slot = place.slot(*out_axes(half, da, db))
        return jnp.dot(
            attb[chunk, half * 128 : (half + 1) * 128],
            wo[:, pl.ds(pl.multiple_of(slot * F, F), F)],
            preferred_element_type=F32,
        )

    ORDER = (2, 1, 3, 0)

    def out_1(chunk):
        for db in ORDER:
            for half in range(2):
                part = out_part(chunk, half, 2, db).astype(BF16)
                for way in range(2):
                    st1[chunk, half, way, db] = part[64 * way : 64 * way + 64]
                    out_copy(chunk, half, way, 0, db).start()
        for da in (1, 3, 0):
            for db in ORDER:
                for half in range(2):
                    parts[chunk, half, da, db] = out_part(chunk, half, da, db)

    def out_2(chunk):
        for db in ORDER:
            for half in range(2):
                for way in range(2):
                    same = slice(64 * way, 64 * way + 64)
                    rest = slice(64 - 64 * way, 128 - 64 * way)
                    da = (1, 3)[way]
                    st2[chunk, half, way, db, rest] = parts[chunk, half, da, db, rest].astype(BF16)
                    out_copy(chunk, half, way, 0, db).wait_recv()
                    part = parts[chunk, half, da, db, same] + rv1[chunk, half, way, db].astype(F32)
                    st2[chunk, half, way, db, same] = part.astype(BF16)
                    out_copy(chunk, half, way, 1, db).start()

    def out_3(chunk):
        for db in ORDER:
            for half in range(2):
                part = parts[chunk, half, 0, db]
                for way in range(2):
                    out_copy(chunk, half, way, 1, db).wait_recv()
                    part = part + rv2[chunk, half, way, db].astype(F32)
                if db == 2:
                    for way in range(2):
                        st3[chunk, half, way] = part[64 * way : 64 * way + 64].astype(BF16)
                        out_copy(chunk, half, way, 2).start()
                else:
                    parts[chunk, half, 0, db] = part

    def out_4(chunk):
        for half in range(2):
            for way in range(2):
                same = slice(64 * way, 64 * way + 64)
                rest = slice(64 - 64 * way, 128 - 64 * way)
                db = (1, 3)[way]
                st4[chunk, half, way, rest] = parts[chunk, half, 0, db, rest].astype(BF16)
                out_copy(chunk, half, way, 2).wait_recv()
                part = parts[chunk, half, 0, db, same] + rv3[chunk, half, way].astype(F32)
                st4[chunk, half, way, same] = part.astype(BF16)
                out_copy(chunk, half, way, 3).start()

    def out_5(chunk):
        for half in range(2):
            part = parts[chunk, half, 0, 0]
            for way in range(2):
                out_copy(chunk, half, way, 3).wait_recv()
                part = part + rv4[chunk, half, way].astype(F32)
            start = chunk * T + half * 128
            out_ref[start : start + 128] = part.astype(BF16)

    def late(m):
        place_of = m + div(m + 14, 15) + div(m, 15)
        chunk = rem(place_of, 2)
        return chunk, div(place_of - 3 * chunk, 2)

    def send_first(chunk, block):
        for head in range(2):
            send_part(chunk, block, head, 0, head)

    def pass_on(chunk, block, step, way):
        for head in range(2):
            have = jnp.logical_or(step > 1, way == head)
            pl.when(have)(lambda head=head: merge_part(chunk, block, way, step - 1, head))
            send_part(chunk, block, way, step, head)

    def complete(chunk, block):
        for head in range(2):
            rows = pl.ds(head * HD, HD)
            for way in range(2):
                merge_part(chunk, block, way, 3, head)
            done = blocks_o[block, rows, :] / blocks_s[block, pl.ds(2 * head + 1, 1), :]
            attb[chunk, :, rows] = done.T.astype(BF16)

    def return_block(m):
        chunk, i = late(m)
        block = chunk * 8 + i
        step, way, _ = sides(i)
        pl.when(i == 0)(lambda: send_first(chunk, block))
        pl.when(jnp.logical_and(i > 0, i < 7))(lambda: pass_on(chunk, block, step, way))
        pl.when(i == 7)(lambda: complete(chunk, block))

    def gain_finish():
        for stage in range(2):
            for d in (1, 2, 3):
                gain_copy(stage, d).wait_send()

    def one_block(m, carry):
        def number(m):
            chunk, i = late(m)
            return chunk * 8 + i

        now, later = number(m), number(rem(m + 1, 16))
        phase(now, 0, now, 1)
        phase(now, 1, later, 0)
        pl.when(m > 0)(lambda: return_block(m - 1))
        pl.when(m == 14)(lambda: out_1(0))
        for at, work in (
            (2, gather_a.finish),
            (3, gather_b.finish),
            (4, gather_e.finish),
            (5, ring_a.finish),
            (6, ring_b.finish),
            (7, gain_finish),
        ):
            pl.when(m == at)(work)
        return carry

    phase(None, 0, 0, 0)
    lax.fori_loop(0, 8 * CHUNKS, one_block, 0)
    out_2(0)
    complete(1, 15)
    out_1(1)
    out_3(0)
    out_2(1)
    out_4(0)
    out_3(1)
    out_5(0)
    out_4(1)
    out_5(1)

    for chunk in range(CHUNKS):
        for way in range(2):
            for step in range(4):
                for half in range(2):
                    if step > 0 or half == way:
                        o_copy(chunk, way, step, half).wait_send()
                    for db in range(4 if step < 2 else 1):
                        out_copy(chunk, half, way, step, db).wait_send()


def per_device(hidden_in, norm_gain, w_query, enc_states, w_key, w_value, w_out, block_counts):
    any_spec = pl.BlockSpec(memory_space=pl.ANY)
    vmem = pltpu.VMEM
    dma = pltpu.SemaphoreType.DMA
    scratch = [
        vmem((HEAD * F, F), BF16),
        vmem((DE, F), BF16),
        vmem((DE, F), BF16),
        vmem((F, HEAD * F), BF16),
        vmem((CHUNKS, HEAD, T, F), BF16),
        vmem((HEAD, BLOCK, DE), BF16),
        vmem((CHUNKS, Z, F, T), BF16),
        vmem((2, KEYS, HD), BF16),
        vmem((F, KEYS), BF16),
        vmem((KEYS, T), F32),
        vmem((KEYS, T), F32),
        vmem((8, T), F32),
        vmem((8, T), F32),
        vmem((CHUNKS * Z, F, T), F32),
        vmem((CHUNKS * Z, 8, T), F32),
        vmem((SLOTS, 8, T), F32),
        vmem((CHUNKS, 2, 4, 2, HD + 16, T), BF16),
        vmem((CHUNKS, 2, 4, 2, HD + 16, T), BF16),
        vmem((CHUNKS, T, F), BF16),
        vmem((CHUNKS, 2, 2, 4, 64, F), BF16),
        vmem((CHUNKS, 2, 2, 4, 64, F), BF16),
        vmem((CHUNKS, 2, 2, 4, 128, F), BF16),
        vmem((CHUNKS, 2, 2, 4, 128, F), BF16),
        vmem((CHUNKS, 2, 2, 64, F), BF16),
        vmem((CHUNKS, 2, 2, 64, F), BF16),
        vmem((CHUNKS, 2, 2, 128, F), BF16),
        vmem((CHUNKS, 2, 2, 128, F), BF16),
        vmem((CHUNKS, 2, 4, 4, 128, F), F32),
        vmem((HEAD, 8, F), F32),
        dma((7,)),
        dma((6,)),
        dma((6,)),
        dma((3, 40)),
        dma((3, 40)),
        dma((CHUNKS * 16,)),
        dma((CHUNKS * 16,)),
        dma((CHUNKS * 16,)),
        dma((CHUNKS * 16,)),
        dma((CHUNKS * 40,)),
        dma((CHUNKS * 40,)),
    ]
    return pl.pallas_call(
        kernel,
        out_shape=jax.ShapeDtypeStruct((CHUNKS * T, F), BF16),
        in_specs=[
            any_spec,
            pl.BlockSpec(memory_space=pltpu.VMEM),
            any_spec,
            any_spec,
            any_spec,
            any_spec,
            any_spec,
            pl.BlockSpec(memory_space=pltpu.SMEM),
        ],
        out_specs=pl.BlockSpec(memory_space=pltpu.VMEM),
        scratch_shapes=scratch,
        compiler_params=pltpu.CompilerParams(
            collective_id=0, has_side_effects=True, vmem_limit_bytes=60 * 1024 * 1024
        ),
        cost_estimate=pl.CostEstimate(
            flops=13_000_000_000, bytes_accessed=8_000_000, transcendentals=17_000_000
        ),
    )(
        hidden_in, norm_gain, w_query, enc_states, w_key, w_value, w_out, block_counts
    )


def solution(mesh):
    placed = (
        P(("dp", "span"), "head"),
        P("head"),
        P(None, "head"),
        P(("dp", "span", "head"), None),
        P(None, "head"),
        P(None, "head"),
        P("head", None),
        P("dp"),
    )
    return jax.shard_map(
        per_device, mesh=mesh, in_specs=placed, out_specs=P(("dp", "span"), "head"), check_vma=False
    )
```

```python
import math

import jax
import jax.numpy as jnp
from jax import lax
from jax.experimental import pallas as pl
from jax.experimental.pallas import tpu as pltpu
from jax.sharding import PartitionSpec as P

HD = 128
X = 4
Y = 4
Z = 8
HEAD = X * Y
T = 256
CHUNKS = 2
F = 256
BLOCK = 128
SLOTS = 16
KEYS = BLOCK * SLOTS
TILE = 256
LAG = 0
DE = 1024
LOG2E = 1.4426950408889634
COEF = LOG2E / math.sqrt(HD)
NEG = -1e30
F32 = jnp.float32
BF16 = jnp.bfloat16
MESH = pl.DeviceIdType.MESH


def div(value, by):
    return value // by if isinstance(value, int) else lax.div(value, by)


def rem(value, by):
    return value % by if isinstance(value, int) else lax.rem(value, by)


def wrap(value, size):
    return rem(value + 2 * size, size)


class Place:
    def __init__(self):
        self.dp = lax.axis_index("dp")
        self.z = lax.axis_index("span")
        self.head = lax.axis_index("head")
        self.x = div(self.head, Y)
        self.y = rem(self.head, Y)

    def slot(self, dx, dy):
        return wrap(self.x + dx, X) * Y + wrap(self.y + dy, Y)

    def at_xy(self, dx, dy):
        return (self.dp, self.z, self.slot(dx, dy))

    def at_z(self, dz):
        return (self.dp, wrap(self.z + dz, Z), self.head)


class Gather:
    REL = (0, -1, 1, 2)

    def __init__(self, place, buf, rows, send, recv):
        self.place, self.buf, self.rows, self.send, self.recv = place, buf, rows, send, recv
        self.started = []

    def shift(self, half, da, db):
        return (db, da) if half == 0 else (da, db)

    def part(self, half, da, db, quarter):
        base = half * (self.rows // 2)
        count = self.rows // 2
        if quarter is not None:
            count = self.rows // 4
            base = base + quarter * count
        return self.buf.at[self.place.slot(*self.shift(half, da, db)), pl.ds(base, count)]

    def copy(self, half, index, ref, to):
        return pltpu.make_async_remote_copy(
            src_ref=ref,
            dst_ref=ref,
            send_sem=self.send.at[half * 20 + index],
            recv_sem=self.recv.at[half * 20 + index],
            device_id=to,
            device_id_type=MESH,
        )

    def sent(self, half, index, da, db, quarter, ta, tb):
        ref = self.part(half, da, db, quarter)
        return self.copy(half, index, ref, self.place.at_xy(*self.shift(half, ta, tb)))

    def go(self, *what):
        self.sent(*what).start()
        self.started.append(what)

    def take(self, half, index, da, db, quarter):
        ref = self.part(half, da, db, quarter)
        self.copy(half, index, ref, self.place.at_xy(1, 0)).wait_recv()

    def line(self, half, which):
        base = 4 + 4 * which
        rel = self.REL[which]
        self.go(half, base, rel, 0, None, 0, 1)
        self.go(half, base + 1, rel, 0, None, 0, -1)

    def pass_on(self, half, which):
        base = 4 + 4 * which
        rel = self.REL[which]
        self.take(half, base, rel, -1, None)
        self.go(half, base + 2, rel, -1, 0, 0, 1)
        self.take(half, base + 1, rel, 1, None)
        self.go(half, base + 3, rel, 1, 1, 0, -1)

    def s0(self):
        for half in range(2):
            self.go(half, 0, 0, 0, None, 1, 0)
            self.go(half, 1, 0, 0, None, -1, 0)
        for half in range(2):
            self.line(half, 0)

    def s1(self):
        for half in range(2):
            self.take(half, 0, -1, 0, None)
            self.go(half, 2, -1, 0, 0, 1, 0)
            self.take(half, 1, 1, 0, None)
            self.go(half, 3, 1, 0, 1, -1, 0)
        for half in range(2):
            self.line(half, 1)
            self.line(half, 2)

    def s2(self):
        for half in range(2):
            self.pass_on(half, 0)

    def s3(self):
        for half in range(2):
            self.take(half, 2, 2, 0, 0)
            self.take(half, 3, 2, 0, 1)
            self.line(half, 3)

    def s4(self):
        for which in (1, 2):
            for half in range(2):
                self.pass_on(half, which)

    def s5(self):
        for half in range(2):
            self.pass_on(half, 3)

    def s6(self):
        for which in range(4):
            for half in range(2):
                base = 4 + 4 * which
                rel = self.REL[which]
                self.take(half, base + 2, rel, 2, 0)
                self.take(half, base + 3, rel, 2, 1)

    def finish(self):
        for what in self.started:
            self.sent(*what).wait_send()


class QueryRing:
    def __init__(self, place, buf, chunk, send, recv):
        self.place, self.buf, self.chunk, self.send, self.recv = place, buf, chunk, send, recv
        self.started = []

    def copy(self, way, step, head, dz):
        ref = self.buf.at[self.chunk, wrap(self.place.z + dz, Z), pl.ds(head * HD, HD)]
        index = ((self.chunk * 2 + way) * 4 + step) * 2 + head
        return pltpu.make_async_remote_copy(
            src_ref=ref,
            dst_ref=ref,
            send_sem=self.send.at[index],
            recv_sem=self.recv.at[index],
            device_id=self.place.at_z(1 - 2 * way),
            device_id_type=MESH,
        )

    def go(self, way, step, head):
        if step == 3 and head != way:
            return
        what = (way, step, head, -step if way == 0 else step)
        self.copy(*what).start()
        self.started.append(what)

    def begin(self):
        for head in range(2):
            for way in range(2):
                self.go(way, 0, head)

    def hop(self, step):
        for head in range(2):
            for way in range(2):
                if step == 3 and head != way:
                    continue
                self.copy(way, step, head, -1 - step if way == 0 else 1 + step).wait_recv()
                if step < 3:
                    self.go(way, step + 1, head)

    def finish(self):
        for what in self.started:
            self.copy(*what).wait_send()


def kernel(
    hidden_hbm, gain_ref, wq_hbm, enc_hbm, wk_hbm, wv_hbm, wo_hbm, count_ref, out_ref,
    wq, wk, wv, wo, nbuf, ebuf, qbuf, kbuf, vbuf, score_0, score_1, best_0, best_1, blocks_o, blocks_s, live_buf,

    osend, orecv, attb,
    st1, rv1, st2, rv2, st3, rv3, parts, gains,
    local_sem, ms_ss, ms_rs, ag_ss, ag_rs, q_ss, q_rs, o_ss, o_rs, x_ss, x_rs,
):
    place = Place()
    me = place.head
    z = place.z

    local = [
        pltpu.make_async_copy(source, target, local_sem.at[index])
        for index, (source, target) in enumerate(
            (
                (hidden_hbm.at[pl.ds(0, T)], nbuf.at[0, me]),
                (hidden_hbm.at[pl.ds(T, T)], nbuf.at[1, me]),
                (enc_hbm, ebuf.at[me]),
                (wq_hbm, wq),
                (wk_hbm, wk),
                (wv_hbm, wv),
                (wo_hbm, wo),
            )
        )
    ]
    for copy in local:
        copy.start()

    barrier = pltpu.get_barrier_semaphore()
    partners = [place.at_xy(d, 0) for d in (1, 2, 3)]
    partners += [place.at_xy(0, d) for d in (1, 2, 3)]
    partners += [place.at_z(1), place.at_z(-1)]
    for partner in partners:
        pl.semaphore_signal(barrier, inc=1, device_id=partner, device_id_type=MESH)

    gains[pl.ds(me, 1)] = jnp.broadcast_to(gain_ref[...].astype(F32).reshape(1, 1, F), (1, 8, F))

    def gain_copy(stage, d, behind=0):
        if stage == 0:
            ref, to = gains.at[place.slot(0, -behind)], place.at_xy(0, d)
        else:
            ref, to = gains.at[pl.ds(wrap(place.x - behind, X) * Y, Y)], place.at_xy(d, 0)
        return pltpu.make_async_remote_copy(
            src_ref=ref,
            dst_ref=ref,
            send_sem=ms_ss.at[stage * 3 + d - 1],
            recv_sem=ms_rs.at[stage * 3 + d - 1],
            device_id=to,
            device_id_type=MESH,
        )

    def gain_go(stage):
        for d in (1, 2, 3):
            gain_copy(stage, d).start()

    def gain_take(stage):
        for d in (1, 2, 3):
            gain_copy(stage, d, d).wait_recv()

    gather_e = Gather(place, ebuf, BLOCK, ag_ss.at[0], ag_rs.at[0])
    gather_a = Gather(place, nbuf.at[0], T, ag_ss.at[1], ag_rs.at[1])
    gather_b = Gather(place, nbuf.at[1], T, ag_ss.at[2], ag_rs.at[2])
    ring_a = QueryRing(place, qbuf, 0, q_ss, q_rs)
    ring_b = QueryRing(place, qbuf, 1, q_ss, q_rs)

    def project(chunk):
        squares = jnp.zeros((T, F), F32)
        for source in range(HEAD):
            rows = nbuf[chunk, source].astype(F32)
            squares = squares + rows * rows
        mean = jnp.sum(squares, axis=1, keepdims=True) * (1.0 / (HEAD * F))
        inverse = lax.rsqrt(mean + 1e-05)
        acc = jnp.zeros((T, F), F32)
        for source in range(HEAD):
            rows = nbuf[chunk, source].astype(F32) * inverse * gains[source, 0:1, :]
            acc = acc + jnp.dot(
                rows.astype(BF16), wq[source * F : (source + 1) * F], preferred_element_type=F32
            )
        qbuf[chunk, pl.ds(z, 1)] = acc.T.astype(BF16)[None]

    live_blocks = count_ref[z]

    def encode():
        for part in range(4):
            rows = ebuf[4 * part : 4 * part + 4].reshape(4 * BLOCK, DE)
            keys = jnp.dot(rows, wk[...], preferred_element_type=F32)
            values = jnp.dot(rows, wv[...], preferred_element_type=F32)
            slot = lax.broadcasted_iota(jnp.int32, (4 * BLOCK, HD), 0) // BLOCK + 4 * part
            live = slot < live_blocks
            span = pl.ds(part * 4 * BLOCK, 4 * BLOCK)
            for head in range(2):
                cols = slice(head * HD, (head + 1) * HD)
                key_block = keys[:, cols]
                lead = key_block[:BLOCK] if part == 0 else kbuf[head, :BLOCK].astype(F32)
                lead = jnp.concatenate([lead] * 4, axis=0)
                kbuf[head, span] = jnp.where(live, key_block, lead).astype(BF16)
                vbuf[cols, span] = jnp.where(live, values[:, cols], 0.0).T.astype(BF16)

    blocks_s[...] = jnp.zeros((CHUNKS * Z, 8, T), F32)
    for slot in range(SLOTS):
        alive = (jnp.zeros((8, T), jnp.int32) + slot) < live_blocks
        live_buf[slot] = jnp.where(alive, 1.0, 0.0)

    pl.semaphore_wait(barrier, len(partners))
    local[0].wait()
    gather_a.s0()
    local[1].wait()
    gather_b.s0()
    gain_go(0)
    gather_a.s1()
    gather_a.s2()
    gain_take(0)
    gain_go(1)
    gather_a.s3()
    gather_b.s1()
    gather_a.s4()
    gather_a.s5()
    gather_b.s2()
    gather_b.s3()
    gather_a.s6()
    gain_take(1)
    local[3].wait()
    project(0)
    ring_a.begin()
    gather_b.s4()
    gather_b.s5()
    local[2].wait()
    gather_e.s0()
    ring_a.hop(0)
    gather_b.s6()
    project(1)
    ring_b.begin()
    ring_a.hop(1)
    gather_e.s1()
    ring_b.hop(0)
    gather_e.s2()
    gather_e.s3()
    ring_a.hop(2)
    ring_b.hop(1)
    gather_e.s4()
    ring_a.hop(3)
    ring_b.hop(2)
    gather_e.s5()
    ring_b.hop(3)
    gather_e.s6()
    local[4].wait()
    local[5].wait()
    encode()
    local[6].wait()

    score_buf = (score_0, score_1)
    best_buf = (best_0, best_1)

    def sides(i):
        step = div(i + 1, 2)
        way = rem(i + 1, 2)
        return step, way, wrap(z + (1 - 2 * way) * (4 - step), Z)

    def phase(soft, soft_head, block, head):
        if block is not None:
            query = qbuf[div(block, 8), sides(rem(block, 8))[2], pl.ds(head * HD, HD), :]
            top = None
        if soft is not None:
            best = best_buf[soft_head][0:1, :]
            acc = jnp.zeros((HD, T), F32)
            total = jnp.zeros((8, T), F32)
        for tile in range(KEYS // TILE):
            span = slice(tile * TILE, (tile + 1) * TILE)
            if block is not None:
                scores = jnp.dot(kbuf[head, span], query, preferred_element_type=F32)
                score_buf[head][span] = scores
                peak = jnp.max(scores.reshape(TILE // 8, 8, T), axis=0)
                top = peak if top is None else jnp.maximum(top, peak)
            if soft is not None:
                weights = jnp.exp2(score_buf[soft_head][span] * COEF - best)
                for inner in range(TILE // BLOCK):
                    rows = weights[inner * BLOCK : (inner + 1) * BLOCK]
                    rows = jnp.sum(rows.reshape(BLOCK // 8, 8, T), axis=0)
                    total = total + rows * live_buf[tile * (TILE // BLOCK) + inner]
                acc = acc + jnp.dot(
                    vbuf[soft_head * HD : (soft_head + 1) * HD, span],
                    weights.astype(BF16),
                    preferred_element_type=F32,
                )
        if block is not None:
            top = jnp.max(top, axis=0, keepdims=True) * COEF
            best_buf[head][...] = jnp.broadcast_to(top, (8, T))
        if soft is not None:
            blocks_o[soft, pl.ds(soft_head * HD, HD)] = acc
            blocks_s[soft, pl.ds(2 * soft_head, 1)] = best
            blocks_s[soft, pl.ds(2 * soft_head + 1, 1)] = jnp.sum(total, axis=0, keepdims=True)

    def split3(value):
        high = value.astype(BF16).astype(F32)
        middle = (value - high).astype(BF16).astype(F32)
        return [high, middle, value - high - middle]

    def o_copy(chunk, way, step, head):
        index = ((chunk * 2 + way) * 4 + step) * 2 + head
        return pltpu.make_async_remote_copy(
            src_ref=osend.at[chunk, way, step, head],
            dst_ref=orecv.at[chunk, way, step, head],
            send_sem=o_ss.at[index],
            recv_sem=o_rs.at[index],
            device_id=(place.dp, wrap(z + 1 - 2 * way, Z), place.head),
            device_id_type=MESH,
        )

    def send_part(chunk, block, way, step, head):
        osend[chunk, way, step, head, :HD] = blocks_o[block, pl.ds(head * HD, HD), :].astype(BF16)
        rows = split3(blocks_s[block, pl.ds(2 * head, 1), :])
        rows += split3(blocks_s[block, pl.ds(2 * head + 1, 1), :])
        rows = jnp.concatenate(rows + [jnp.zeros((10, T), F32)], axis=0)
        osend[chunk, way, step, head, HD:] = rows.astype(BF16)
        o_copy(chunk, way, step, head).start()

    def merge_part(chunk, block, way, step, head):
        o_copy(chunk, way, step, head).wait_recv()
        rows = pl.ds(head * HD, HD)
        best_row = pl.ds(2 * head, 1)
        sum_row = pl.ds(2 * head + 1, 1)
        stats = orecv[chunk, way, step, head, HD:, :].astype(F32)
        best_a = blocks_s[block, best_row, :]
        best_b = stats[0:1] + stats[1:2] + stats[2:3]
        sum_b = stats[3:4] + stats[4:5] + stats[5:6]
        best = jnp.maximum(best_a, best_b)
        scale_a = jnp.exp2(best_a - best)
        scale_b = jnp.exp2(best_b - best)
        blocks_s[block, best_row] = best
        blocks_s[block, sum_row] = blocks_s[block, sum_row, :] * scale_a + sum_b * scale_b
        blocks_o[block, rows] = (
            blocks_o[block, rows, :] * scale_a
            + orecv[chunk, way, step, head, :HD, :].astype(F32) * scale_b
        )

    def out_axes(half, da, db):
        return (da, db) if half == 0 else (db, da)

    def out_copy(chunk, half, way, step, db=0):
        if step < 2:
            send, recv = ((st1, rv1), (st2, rv2))[step]
            source, target = send.at[chunk, half, way, db], recv.at[chunk, half, way, db]
            to = place.at_xy(*out_axes(half, 1 - 2 * way, 0))
            index = ((chunk * 2 + half) * 2 + way) * 8 + step * 4 + db
        else:
            source, target = st3.at[chunk, half, db - 1], rv3.at[chunk, half, db - 1]
            to = place.at_xy(*out_axes(half, 0, db))
            index = CHUNKS * 32 + (chunk * 2 + half) * 3 + db - 1
        return pltpu.make_async_remote_copy(
            src_ref=source,
            dst_ref=target,
            send_sem=x_ss.at[index],
            recv_sem=x_rs.at[index],
            device_id=to,
            device_id_type=MESH,
        )

    def out_part(chunk, half, da, db):
        slot = place.slot(*out_axes(half, da, db))
        return jnp.dot(
            attb[chunk, half * 128 : (half + 1) * 128],
            wo[:, pl.ds(pl.multiple_of(slot * F, F), F)],
            preferred_element_type=F32,
        )

    ORDER = (2, 1, 3, 0)

    def out_1(chunk):
        for db in ORDER:
            for half in range(2):
                part = out_part(chunk, half, 2, db).astype(BF16)
                for way in range(2):
                    st1[chunk, half, way, db] = part[64 * way : 64 * way + 64]
                    out_copy(chunk, half, way, 0, db).start()
        for da in (1, 3, 0):
            for db in ORDER:
                for half in range(2):
                    parts[chunk, half, da, db] = out_part(chunk, half, da, db)

    def out_2(chunk):
        for db in ORDER:
            for half in range(2):
                for way in range(2):
                    same = slice(64 * way, 64 * way + 64)
                    rest = slice(64 - 64 * way, 128 - 64 * way)
                    da = (1, 3)[way]
                    st2[chunk, half, way, db, rest] = parts[chunk, half, da, db, rest].astype(BF16)
                    out_copy(chunk, half, way, 0, db).wait_recv()
                    part = parts[chunk, half, da, db, same] + rv1[chunk, half, way, db].astype(F32)
                    st2[chunk, half, way, db, same] = part.astype(BF16)
                    out_copy(chunk, half, way, 1, db).start()

    def out_3(chunk):
        for db in ORDER:
            for half in range(2):
                part = parts[chunk, half, 0, db]
                for way in range(2):
                    out_copy(chunk, half, way, 1, db).wait_recv()
                    part = part + rv2[chunk, half, way, db].astype(F32)
                if db > 0:
                    st3[chunk, half, db - 1] = part.astype(BF16)
                    out_copy(chunk, half, 0, 2, db).start()
                else:
                    parts[chunk, half, 0, 0] = part

    def out_4(chunk):
        for half in range(2):
            part = parts[chunk, half, 0, 0]
            for db in (1, 3, 2):
                out_copy(chunk, half, 0, 2, db).wait_recv()
                part = part + rv3[chunk, half, db - 1].astype(F32)
            start = chunk * T + half * 128
            out_ref[start : start + 128] = part.astype(BF16)

    def late(m):
        begun = div(m + 16 - LAG, 16)
        ending = div(m + LAG, 16)
        both = begun * (1 - ending)
        k = m - LAG + 16
        odd = rem(k, 2)
        i = (1 - begun) * m + both * (div(k, 2) - 8 + LAG * (1 - odd)) + ending * (m - 8)
        return both * odd + ending, i

    def pass_on(chunk, block, step, way, head):
        have = jnp.logical_or(step > 1, way == head)
        pl.when(have)(lambda: merge_part(chunk, block, way, step - 1, head))
        send_part(chunk, block, way, step, head)

    def complete(chunk, block, head):
        rows = pl.ds(head * HD, HD)
        for way in range(2):
            merge_part(chunk, block, way, 3, head)
        done = blocks_o[block, rows, :] / blocks_s[block, pl.ds(2 * head + 1, 1), :]
        attb[chunk, :, rows] = done.T.astype(BF16)

    def return_part(m, head):
        chunk, i = late(m)
        block = chunk * 8 + i
        step, way, _ = sides(i)
        inner = jnp.logical_and(i > 0, i < 7)
        pl.when(inner)(lambda: pass_on(chunk, block, step, way, head))
        pl.when(i == 7)(lambda: complete(chunk, block, head))

    def gain_finish():
        for stage in range(2):
            for d in (1, 2, 3):
                gain_copy(stage, d).wait_send()

    def one_block(m, carry):
        def number(m):
            chunk, i = late(m)
            return chunk * 8 + i

        now, later = number(m), number(rem(m + 1, 16))
        phase(now, 0, now, 1)
        pl.when(rem(now, 8) == 0)(lambda: send_part(div(now, 8), now, 0, 0, 0))
        pl.when(m > 0)(lambda: return_part(m - 1, 0))
        phase(now, 1, later, 0)
        pl.when(rem(now, 8) == 0)(lambda: send_part(div(now, 8), now, 1, 0, 1))
        pl.when(m > 0)(lambda: return_part(m - 1, 1))
        pl.when(m == 15)(lambda: out_1(0))
        for at, work in (
            (2, gather_a.finish),
            (3, gather_b.finish),
            (4, gather_e.finish),
            (5, ring_a.finish),
            (6, ring_b.finish),
            (7, gain_finish),
        ):
            pl.when(m == at)(work)
        return carry

    phase(None, 0, 0, 0)
    lax.fori_loop(0, 8 * CHUNKS, one_block, 0)
    for head in range(2):
        complete(1, 15, head)
    out_1(1)
    out_2(0)
    out_2(1)
    out_3(0)
    out_3(1)
    out_4(0)
    out_4(1)

    for chunk in range(CHUNKS):
        for way in range(2):
            for step in range(4):
                for half in range(2):
                    if step > 0 or half == way:
                        o_copy(chunk, way, step, half).wait_send()
                    for db in range(4):
                        if step < 2 or (step == 2 and way == 0 and db > 0):
                            out_copy(chunk, half, way, step, db).wait_send()


def per_device(hidden_in, norm_gain, w_query, enc_states, w_key, w_value, w_out, block_counts):
    any_spec = pl.BlockSpec(memory_space=pl.ANY)
    vmem = pltpu.VMEM
    dma = pltpu.SemaphoreType.DMA
    scratch = [
        vmem((HEAD * F, F), BF16),
        vmem((DE, F), BF16),
        vmem((DE, F), BF16),
        vmem((F, HEAD * F), BF16),
        vmem((CHUNKS, HEAD, T, F), BF16),
        vmem((HEAD, BLOCK, DE), BF16),
        vmem((CHUNKS, Z, F, T), BF16),
        vmem((2, KEYS, HD), BF16),
        vmem((F, KEYS), BF16),
        vmem((KEYS, T), F32),
        vmem((KEYS, T), F32),
        vmem((8, T), F32),
        vmem((8, T), F32),
        vmem((CHUNKS * Z, F, T), F32),
        vmem((CHUNKS * Z, 8, T), F32),
        vmem((SLOTS, 8, T), F32),
        vmem((CHUNKS, 2, 4, 2, HD + 16, T), BF16),
        vmem((CHUNKS, 2, 4, 2, HD + 16, T), BF16),
        vmem((CHUNKS, T, F), BF16),
        vmem((CHUNKS, 2, 2, 4, 64, F), BF16),
        vmem((CHUNKS, 2, 2, 4, 64, F), BF16),
        vmem((CHUNKS, 2, 2, 4, 128, F), BF16),
        vmem((CHUNKS, 2, 2, 4, 128, F), BF16),
        vmem((CHUNKS, 2, 3, 128, F), BF16),
        vmem((CHUNKS, 2, 3, 128, F), BF16),
        vmem((CHUNKS, 2, 4, 4, 128, F), F32),
        vmem((HEAD, 8, F), F32),
        dma((7,)),
        dma((6,)),
        dma((6,)),
        dma((3, 40)),
        dma((3, 40)),
        dma((CHUNKS * 16,)),
        dma((CHUNKS * 16,)),
        dma((CHUNKS * 16,)),
        dma((CHUNKS * 16,)),
        dma((CHUNKS * 38,)),
        dma((CHUNKS * 38,)),
    ]
    return pl.pallas_call(
        kernel,
        out_shape=jax.ShapeDtypeStruct((CHUNKS * T, F), BF16),
        in_specs=[
            any_spec,
            pl.BlockSpec(memory_space=pltpu.VMEM),
            any_spec,
            any_spec,
            any_spec,
            any_spec,
            any_spec,
            pl.BlockSpec(memory_space=pltpu.SMEM),
        ],
        out_specs=pl.BlockSpec(memory_space=pltpu.VMEM),
        scratch_shapes=scratch,
        compiler_params=pltpu.CompilerParams(
            collective_id=0, has_side_effects=True, vmem_limit_bytes=60 * 1024 * 1024
        ),
        cost_estimate=pl.CostEstimate(
            flops=13_000_000_000, bytes_accessed=8_000_000, transcendentals=17_000_000
        ),
    )(
        hidden_in, norm_gain, w_query, enc_states, w_key, w_value, w_out, block_counts
    )


def solution(mesh):
    placed = (
        P(("dp", "span"), "head"),
        P("head"),
        P(None, "head"),
        P(("dp", "span", "head"), None),
        P(None, "head"),
        P(None, "head"),
        P("head", None),
        P("dp"),
    )
    return jax.shard_map(
        per_device, mesh=mesh, in_specs=placed, out_specs=P(("dp", "span"), "head"), check_vma=False
    )
```

```python
import math

import jax
import jax.numpy as jnp
from jax import lax
from jax.experimental import pallas as pl
from jax.experimental.pallas import tpu as pltpu
from jax.sharding import PartitionSpec as P

HD = 128
X = 4
Y = 4
Z = 8
HEAD = X * Y
T = 256
CHUNKS = 2
F = 256
BLOCK = 128
SLOTS = 16
KEYS = BLOCK * SLOTS
TILE = 256
FIRST = 0
BLOCK_ORDER = (0, 1, 2, 8, 9, 10, 3, 4, 11, 12, 5, 6, 13, 14, 7, 15)
DE = 1024
LOG2E = 1.4426950408889634
COEF = LOG2E / math.sqrt(HD)
NEG = -1e30
F32 = jnp.float32
BF16 = jnp.bfloat16
MESH = pl.DeviceIdType.MESH


def div(value, by):
    return value // by if isinstance(value, int) else lax.div(value, by)


def rem(value, by):
    return value % by if isinstance(value, int) else lax.rem(value, by)


def wrap(value, size):
    return rem(value + 2 * size, size)


class Place:
    def __init__(self):
        self.dp = lax.axis_index("dp")
        self.z = lax.axis_index("span")
        self.head = lax.axis_index("head")
        self.x = div(self.head, Y)
        self.y = rem(self.head, Y)

    def slot(self, dx, dy):
        return wrap(self.x + dx, X) * Y + wrap(self.y + dy, Y)

    def at_xy(self, dx, dy):
        return (self.dp, self.z, self.slot(dx, dy))

    def at_z(self, dz):
        return (self.dp, wrap(self.z + dz, Z), self.head)


class Gather:
    REL = (0, -1, 1, 2)

    def __init__(self, place, buf, rows, send, recv):
        self.place, self.buf, self.rows, self.send, self.recv = place, buf, rows, send, recv
        self.started = []

    def shift(self, half, da, db):
        return (db, da) if half == 0 else (da, db)

    def part(self, half, da, db, quarter):
        base = half * (self.rows // 2)
        count = self.rows // 2
        if quarter is not None:
            count = self.rows // 4
            base = base + quarter * count
        return self.buf.at[self.place.slot(*self.shift(half, da, db)), pl.ds(base, count)]

    def copy(self, half, index, ref, to):
        return pltpu.make_async_remote_copy(
            src_ref=ref,
            dst_ref=ref,
            send_sem=self.send.at[half * 20 + index],
            recv_sem=self.recv.at[half * 20 + index],
            device_id=to,
            device_id_type=MESH,
        )

    def sent(self, half, index, da, db, quarter, ta, tb):
        ref = self.part(half, da, db, quarter)
        return self.copy(half, index, ref, self.place.at_xy(*self.shift(half, ta, tb)))

    def go(self, *what):
        self.sent(*what).start()
        self.started.append(what)

    def take(self, half, index, da, db, quarter):
        ref = self.part(half, da, db, quarter)
        self.copy(half, index, ref, self.place.at_xy(1, 0)).wait_recv()

    def line(self, half, which):
        base = 4 + 4 * which
        rel = self.REL[which]
        self.go(half, base, rel, 0, None, 0, 1)
        self.go(half, base + 1, rel, 0, None, 0, -1)

    def pass_on(self, half, which):
        base = 4 + 4 * which
        rel = self.REL[which]
        self.take(half, base, rel, -1, None)
        self.go(half, base + 2, rel, -1, 0, 0, 1)
        self.take(half, base + 1, rel, 1, None)
        self.go(half, base + 3, rel, 1, 1, 0, -1)

    def s0(self):
        for half in range(2):
            self.go(half, 0, 0, 0, None, 1, 0)
            self.go(half, 1, 0, 0, None, -1, 0)
        for half in range(2):
            self.line(half, 0)

    def s1(self):
        for half in range(2):
            self.take(half, 0, -1, 0, None)
            self.go(half, 2, -1, 0, 0, 1, 0)
            self.take(half, 1, 1, 0, None)
            self.go(half, 3, 1, 0, 1, -1, 0)
        for half in range(2):
            self.line(half, 1)
            self.line(half, 2)

    def s2(self):
        for half in range(2):
            self.pass_on(half, 0)

    def s3(self):
        for half in range(2):
            self.take(half, 2, 2, 0, 0)
            self.take(half, 3, 2, 0, 1)
            self.line(half, 3)

    def s4(self):
        for which in (1, 2):
            for half in range(2):
                self.pass_on(half, which)

    def s5(self):
        for half in range(2):
            self.pass_on(half, 3)

    def s6(self):
        for which in range(4):
            for half in range(2):
                base = 4 + 4 * which
                rel = self.REL[which]
                self.take(half, base + 2, rel, 2, 0)
                self.take(half, base + 3, rel, 2, 1)

    def finish(self):
        for what in self.started:
            self.sent(*what).wait_send()


class QueryRing:
    def __init__(self, place, buf, chunk, send, recv):
        self.place, self.buf, self.chunk, self.send, self.recv = place, buf, chunk, send, recv
        self.started = []

    def copy(self, way, step, head, dz):
        ref = self.buf.at[self.chunk, wrap(self.place.z + dz, Z), pl.ds(head * HD, HD)]
        index = ((self.chunk * 2 + way) * 4 + step) * 2 + head
        return pltpu.make_async_remote_copy(
            src_ref=ref,
            dst_ref=ref,
            send_sem=self.send.at[index],
            recv_sem=self.recv.at[index],
            device_id=self.place.at_z(1 - 2 * way),
            device_id_type=MESH,
        )

    def go(self, way, step, head):
        if step == 3 and head != way:
            return
        what = (way, step, head, -step if way == 0 else step)
        self.copy(*what).start()
        self.started.append(what)

    def begin(self):
        for head in range(2):
            for way in range(2):
                self.go(way, 0, head)

    def hop(self, step):
        for head in range(2):
            for way in range(2):
                if step == 3 and head != way:
                    continue
                self.copy(way, step, head, -1 - step if way == 0 else 1 + step).wait_recv()
                if step < 3:
                    self.go(way, step + 1, head)

    def finish(self):
        for what in self.started:
            self.copy(*what).wait_send()


def kernel(
    hidden_hbm, gain_ref, wq_hbm, enc_hbm, wk_hbm, wv_hbm, wo_hbm, count_ref, out_ref,
    wq, wk, wv, wo, nbuf, ebuf, qbuf, kbuf, vbuf, score_0, score_1, best_0, best_1, blocks_o, blocks_s, live_buf,

    osend, orecv, attb,
    st1, rv1, st2, rv2, st3, rv3, parts, gains,
    local_sem, ms_ss, ms_rs, ag_ss, ag_rs, q_ss, q_rs, o_ss, o_rs, x_ss, x_rs,
):
    place = Place()
    me = place.head
    z = place.z

    local = [
        pltpu.make_async_copy(source, target, local_sem.at[index])
        for index, (source, target) in enumerate(
            (
                (hidden_hbm.at[pl.ds(0, T)], nbuf.at[0, me]),
                (hidden_hbm.at[pl.ds(T, T)], nbuf.at[1, me]),
                (enc_hbm, ebuf.at[me]),
                (wq_hbm, wq),
                (wk_hbm, wk),
                (wv_hbm, wv),
                (wo_hbm, wo),
            )
        )
    ]
    for copy in local:
        copy.start()

    barrier = pltpu.get_barrier_semaphore()
    partners = [place.at_xy(d, 0) for d in (1, 2, 3)]
    partners += [place.at_xy(0, d) for d in (1, 2, 3)]
    partners += [place.at_z(d) for d in (1, -1, 2, -2)]
    for partner in partners:
        pl.semaphore_signal(barrier, inc=1, device_id=partner, device_id_type=MESH)

    gains[pl.ds(me, 1)] = jnp.broadcast_to(gain_ref[...].astype(F32).reshape(1, 1, F), (1, 8, F))

    def gain_copy(stage, d, behind=0):
        if stage == 0:
            ref, to = gains.at[place.slot(0, -behind)], place.at_xy(0, d)
        else:
            ref, to = gains.at[pl.ds(wrap(place.x - behind, X) * Y, Y)], place.at_xy(d, 0)
        return pltpu.make_async_remote_copy(
            src_ref=ref,
            dst_ref=ref,
            send_sem=ms_ss.at[stage * 3 + d - 1],
            recv_sem=ms_rs.at[stage * 3 + d - 1],
            device_id=to,
            device_id_type=MESH,
        )

    def gain_go(stage):
        for d in (1, 2, 3):
            gain_copy(stage, d).start()

    def gain_take(stage):
        for d in (1, 2, 3):
            gain_copy(stage, d, d).wait_recv()

    gather_e = Gather(place, ebuf, BLOCK, ag_ss.at[0], ag_rs.at[0])
    gather_a = Gather(place, nbuf.at[0], T, ag_ss.at[1], ag_rs.at[1])
    gather_b = Gather(place, nbuf.at[1], T, ag_ss.at[2], ag_rs.at[2])
    ring_a = QueryRing(place, qbuf, 0, q_ss, q_rs)
    ring_b = QueryRing(place, qbuf, 1, q_ss, q_rs)

    def project(chunk):
        squares = jnp.zeros((T, F), F32)
        for source in range(HEAD):
            rows = nbuf[chunk, source].astype(F32)
            squares = squares + rows * rows
        mean = jnp.sum(squares, axis=1, keepdims=True) * (1.0 / (HEAD * F))
        inverse = lax.rsqrt(mean + 1e-05)
        acc = jnp.zeros((T, F), F32)
        for source in range(HEAD):
            rows = nbuf[chunk, source].astype(F32) * inverse * gains[source, 0:1, :]
            acc = acc + jnp.dot(
                rows.astype(BF16), wq[source * F : (source + 1) * F], preferred_element_type=F32
            )
        qbuf[chunk, pl.ds(z, 1)] = acc.T.astype(BF16)[None]

    live_blocks = count_ref[z]

    def encode():
        for part in range(4):
            rows = ebuf[4 * part : 4 * part + 4].reshape(4 * BLOCK, DE)
            keys = jnp.dot(rows, wk[...], preferred_element_type=F32)
            values = jnp.dot(rows, wv[...], preferred_element_type=F32)
            slot = lax.broadcasted_iota(jnp.int32, (4 * BLOCK, HD), 0) // BLOCK + 4 * part
            live = slot < live_blocks
            span = pl.ds(part * 4 * BLOCK, 4 * BLOCK)
            for head in range(2):
                cols = slice(head * HD, (head + 1) * HD)
                key_block = keys[:, cols]
                lead = key_block[:BLOCK] if part == 0 else kbuf[head, :BLOCK].astype(F32)
                lead = jnp.concatenate([lead] * 4, axis=0)
                kbuf[head, span] = jnp.where(live, key_block, lead).astype(BF16)
                vbuf[cols, span] = jnp.where(live, values[:, cols], 0.0).T.astype(BF16)

    blocks_s[...] = jnp.zeros((CHUNKS * Z, 8, T), F32)
    for slot in range(SLOTS):
        alive = (jnp.zeros((8, T), jnp.int32) + slot) < live_blocks
        live_buf[slot] = jnp.where(alive, 1.0, 0.0)

    pl.semaphore_wait(barrier, len(partners))
    local[0].wait()
    gather_a.s0()
    local[1].wait()
    gather_b.s0()
    gain_go(0)
    gather_a.s1()
    gather_a.s2()
    gain_take(0)
    gain_go(1)
    gather_a.s3()
    gather_b.s1()
    gather_a.s4()
    gather_a.s5()
    gather_b.s2()
    gather_b.s3()
    gather_a.s6()
    gain_take(1)
    local[3].wait()
    project(0)
    ring_a.begin()
    gather_b.s4()
    gather_b.s5()
    local[2].wait()
    gather_e.s0()
    ring_a.hop(0)
    gather_b.s6()
    project(1)
    ring_b.begin()
    ring_a.hop(1)
    gather_e.s1()
    ring_b.hop(0)
    gather_e.s2()
    gather_e.s3()
    ring_a.hop(2)
    ring_b.hop(1)
    gather_e.s4()
    ring_a.hop(3)
    ring_b.hop(2)
    gather_e.s5()
    ring_b.hop(3)
    gather_e.s6()
    local[4].wait()
    local[5].wait()
    encode()
    local[6].wait()

    score_buf = (score_0, score_1)
    best_buf = (best_0, best_1)

    def sides(i):
        step = div(i + 1, 2)
        way = rem(i + 1, 2)
        return step, way, wrap(z + (1 - 2 * way) * (4 - step), Z)

    def phase(soft, soft_head, block, head):
        if block is not None:
            query = qbuf[div(block, 8), sides(rem(block, 8))[2], pl.ds(head * HD, HD), :]
            top = None
        if soft is not None:
            best = best_buf[soft_head][0:1, :]
            acc = jnp.zeros((HD, T), F32)
            total = jnp.zeros((8, T), F32)
        for tile in range(KEYS // TILE):
            span = slice(tile * TILE, (tile + 1) * TILE)
            if block is not None:
                scores = jnp.dot(kbuf[head, span], query, preferred_element_type=F32)
                score_buf[head][span] = scores
                peak = jnp.max(scores.reshape(TILE // 8, 8, T), axis=0)
                top = peak if top is None else jnp.maximum(top, peak)
            if soft is not None:
                weights = jnp.exp2(score_buf[soft_head][span] * COEF - best)
                for inner in range(TILE // BLOCK):
                    rows = weights[inner * BLOCK : (inner + 1) * BLOCK]
                    rows = jnp.sum(rows.reshape(BLOCK // 8, 8, T), axis=0)
                    total = total + rows * live_buf[tile * (TILE // BLOCK) + inner]
                acc = acc + jnp.dot(
                    vbuf[soft_head * HD : (soft_head + 1) * HD, span],
                    weights.astype(BF16),
                    preferred_element_type=F32,
                )
        if block is not None:
            top = jnp.max(top, axis=0, keepdims=True) * COEF
            best_buf[head][...] = jnp.broadcast_to(top, (8, T))
        if soft is not None:
            blocks_o[soft, pl.ds(soft_head * HD, HD)] = acc
            blocks_s[soft, pl.ds(2 * soft_head, 1)] = best
            blocks_s[soft, pl.ds(2 * soft_head + 1, 1)] = jnp.sum(total, axis=0, keepdims=True)

    def split3(value):
        high = value.astype(BF16).astype(F32)
        middle = (value - high).astype(BF16).astype(F32)
        return [high, middle, value - high - middle]

    def o_copy(chunk, way, step, head):
        index = ((chunk * 2 + way) * 4 + step) * 2 + head
        return pltpu.make_async_remote_copy(
            src_ref=osend.at[chunk, way, step, head],
            dst_ref=orecv.at[chunk, way, step, head],
            send_sem=o_ss.at[index],
            recv_sem=o_rs.at[index],
            device_id=(place.dp, wrap(z + (1 - 2 * way) * (2 if step is FIRST else 1), Z), place.head),
            device_id_type=MESH,
        )

    def held(block, head):
        return (
            blocks_o[block, pl.ds(head * HD, HD), :],
            blocks_s[block, pl.ds(2 * head, 1), :],
            blocks_s[block, pl.ds(2 * head + 1, 1), :],
        )

    def send_part(chunk, way, step, head, part):
        values, best, total = part
        osend[chunk, way, step, head, :HD] = values.astype(BF16)
        rows = split3(best) + split3(total) + [jnp.zeros((10, T), F32)]
        osend[chunk, way, step, head, HD:] = jnp.concatenate(rows, axis=0).astype(BF16)
        o_copy(chunk, way, step, head).start()

    def merge_part(chunk, way, step, head, part):
        o_copy(chunk, way, step, head).wait_recv()
        values, best_a, total = part
        stats = orecv[chunk, way, step, head, HD:, :].astype(F32)
        best_b = stats[0:1] + stats[1:2] + stats[2:3]
        total_b = stats[3:4] + stats[4:5] + stats[5:6]
        best = jnp.maximum(best_a, best_b)
        scale_a = jnp.exp2(best_a - best)
        scale_b = jnp.exp2(best_b - best)
        values = values * scale_a + orecv[chunk, way, step, head, :HD, :].astype(F32) * scale_b
        return values, best, total * scale_a + total_b * scale_b

    def out_axes(half, da, db):
        return (da, db) if half == 0 else (db, da)

    def out_copy(chunk, half, way, step, db=0):
        if step < 2:
            send, recv = ((st1, rv1), (st2, rv2))[step]
            source, target = send.at[chunk, half, way, db], recv.at[chunk, half, way, db]
            to = place.at_xy(*out_axes(half, 1 - 2 * way, 0))
            index = ((chunk * 2 + half) * 2 + way) * 8 + step * 4 + db
        else:
            source, target = st3.at[chunk, half, db - 1], rv3.at[chunk, half, db - 1]
            to = place.at_xy(*out_axes(half, 0, db))
            index = CHUNKS * 32 + (chunk * 2 + half) * 3 + db - 1
        return pltpu.make_async_remote_copy(
            src_ref=source,
            dst_ref=target,
            send_sem=x_ss.at[index],
            recv_sem=x_rs.at[index],
            device_id=to,
            device_id_type=MESH,
        )

    def out_part(chunk, half, da, db):
        slot = place.slot(*out_axes(half, da, db))
        return jnp.dot(
            attb[chunk, half * 128 : (half + 1) * 128],
            wo[:, pl.ds(pl.multiple_of(slot * F, F), F)],
            preferred_element_type=F32,
        )

    ORDER = (2, 1, 3, 0)

    def out_1(chunk):
        for db in ORDER:
            for half in range(2):
                part = out_part(chunk, half, 2, db).astype(BF16)
                for way in range(2):
                    st1[chunk, half, way, db] = part[64 * way : 64 * way + 64]
                    out_copy(chunk, half, way, 0, db).start()
        for da in (1, 3, 0):
            for db in ORDER:
                for half in range(2):
                    parts[chunk, half, da, db] = out_part(chunk, half, da, db)

    def out_2(chunk):
        for db in ORDER:
            for half in range(2):
                for way in range(2):
                    same = slice(64 * way, 64 * way + 64)
                    rest = slice(64 - 64 * way, 128 - 64 * way)
                    da = (1, 3)[way]
                    st2[chunk, half, way, db, rest] = parts[chunk, half, da, db, rest].astype(BF16)
                    out_copy(chunk, half, way, 0, db).wait_recv()
                    part = parts[chunk, half, da, db, same] + rv1[chunk, half, way, db].astype(F32)
                    st2[chunk, half, way, db, same] = part.astype(BF16)
                    out_copy(chunk, half, way, 1, db).start()

    def out_3(chunk):
        for db in ORDER:
            for half in range(2):
                part = parts[chunk, half, 0, db]
                for way in range(2):
                    out_copy(chunk, half, way, 1, db).wait_recv()
                    part = part + rv2[chunk, half, way, db].astype(F32)
                if db > 0:
                    st3[chunk, half, db - 1] = part.astype(BF16)
                    out_copy(chunk, half, 0, 2, db).start()
                else:
                    parts[chunk, half, 0, 0] = part

    def out_4(chunk):
        for half in range(2):
            part = parts[chunk, half, 0, 0]
            for db in (1, 3, 2):
                out_copy(chunk, half, 0, 2, db).wait_recv()
                part = part + rv3[chunk, half, db - 1].astype(F32)
            start = chunk * T + half * 128
            out_ref[start : start + 128] = part.astype(BF16)

    def number(m):
        block = BLOCK_ORDER[0]
        for at in range(1, 16):
            block = block + div(m + 16 - at, 16) * (BLOCK_ORDER[at] - BLOCK_ORDER[at - 1])
        return block

    def send_first(block, head):
        i = rem(block, 8)
        chunk = div(block, 8)
        pl.when(i == 0)(lambda: send_part(chunk, head, FIRST, head, held(block, head)))
        pl.when(jnp.logical_and(i > 0, i < 3))(
            lambda: send_part(chunk, rem(i + 1, 2), 1, head, held(block, head))
        )

    def pass_on(chunk, block, step, way, head):
        both = jnp.logical_and(step == 2, way == head)

        @pl.when(both)
        def _():
            part = merge_part(chunk, way, FIRST, head, held(block, head))
            part = merge_part(chunk, way, 1, head, part)
            send_part(chunk, way, 2, head, part)

        @pl.when(jnp.logical_not(both))
        def _():
            part = merge_part(chunk, way, step - 1, head, held(block, head))
            send_part(chunk, way, step, head, part)

    def complete(chunk, block, head):
        part = held(block, head)
        for way in range(2):
            part = merge_part(chunk, way, 3, head, part)
        attb[chunk, :, pl.ds(head * HD, HD)] = (part[0] / part[2]).T.astype(BF16)

    def return_part(m, head):
        block = number(m)
        chunk, i = div(block, 8), rem(block, 8)
        step, way, _ = sides(i)
        inner = jnp.logical_and(i > 2, i < 7)
        pl.when(inner)(lambda: pass_on(chunk, block, step, way, head))
        pl.when(i == 7)(lambda: complete(chunk, block, head))

    def gain_finish():
        for stage in range(2):
            for d in (1, 2, 3):
                gain_copy(stage, d).wait_send()

    def one_block(m, carry):
        now, later = number(m), number(rem(m + 1, 16))
        phase(now, 0, now, 1)
        send_first(now, 0)
        pl.when(m > 0)(lambda: return_part(m - 1, 0))
        phase(now, 1, later, 0)
        send_first(now, 1)
        pl.when(m > 0)(lambda: return_part(m - 1, 1))
        pl.when(m == 15)(lambda: out_1(0))
        for at, work in (
            (2, gather_a.finish),
            (3, gather_b.finish),
            (4, gather_e.finish),
            (5, ring_a.finish),
            (6, ring_b.finish),
            (7, gain_finish),
        ):
            pl.when(m == at)(work)
        return carry

    phase(None, 0, 0, 0)
    lax.fori_loop(0, 8 * CHUNKS, one_block, 0)
    for head in range(2):
        complete(1, 15, head)
    out_1(1)
    out_2(0)
    out_2(1)
    out_3(0)
    out_3(1)
    out_4(0)
    out_4(1)

    for chunk in range(CHUNKS):
        for way in range(2):
            for step in range(4):
                for half in range(2):
                    if step > 0 or half == way:
                        o_copy(chunk, way, step, half).wait_send()
                    for db in range(4):
                        if step < 2 or (step == 2 and way == 0 and db > 0):
                            out_copy(chunk, half, way, step, db).wait_send()


def per_device(hidden_in, norm_gain, w_query, enc_states, w_key, w_value, w_out, block_counts):
    any_spec = pl.BlockSpec(memory_space=pl.ANY)
    vmem = pltpu.VMEM
    dma = pltpu.SemaphoreType.DMA
    scratch = [
        vmem((HEAD * F, F), BF16),
        vmem((DE, F), BF16),
        vmem((DE, F), BF16),
        vmem((F, HEAD * F), BF16),
        vmem((CHUNKS, HEAD, T, F), BF16),
        vmem((HEAD, BLOCK, DE), BF16),
        vmem((CHUNKS, Z, F, T), BF16),
        vmem((2, KEYS, HD), BF16),
        vmem((F, KEYS), BF16),
        vmem((KEYS, T), F32),
        vmem((KEYS, T), F32),
        vmem((8, T), F32),
        vmem((8, T), F32),
        vmem((CHUNKS * Z, F, T), F32),
        vmem((CHUNKS * Z, 8, T), F32),
        vmem((SLOTS, 8, T), F32),
        vmem((CHUNKS, 2, 4, 2, HD + 16, T), BF16),
        vmem((CHUNKS, 2, 4, 2, HD + 16, T), BF16),
        vmem((CHUNKS, T, F), BF16),
        vmem((CHUNKS, 2, 2, 4, 64, F), BF16),
        vmem((CHUNKS, 2, 2, 4, 64, F), BF16),
        vmem((CHUNKS, 2, 2, 4, 128, F), BF16),
        vmem((CHUNKS, 2, 2, 4, 128, F), BF16),
        vmem((CHUNKS, 2, 3, 128, F), BF16),
        vmem((CHUNKS, 2, 3, 128, F), BF16),
        vmem((CHUNKS, 2, 4, 4, 128, F), F32),
        vmem((HEAD, 8, F), F32),
        dma((7,)),
        dma((6,)),
        dma((6,)),
        dma((3, 40)),
        dma((3, 40)),
        dma((CHUNKS * 16,)),
        dma((CHUNKS * 16,)),
        dma((CHUNKS * 16,)),
        dma((CHUNKS * 16,)),
        dma((CHUNKS * 38,)),
        dma((CHUNKS * 38,)),
    ]
    return pl.pallas_call(
        kernel,
        out_shape=pltpu.VMEM((CHUNKS * T, F), BF16),
        in_specs=[
            any_spec,
            pl.BlockSpec(memory_space=pltpu.VMEM),
            any_spec,
            any_spec,
            any_spec,
            any_spec,
            any_spec,
            pl.BlockSpec(memory_space=pltpu.SMEM),
        ],
        out_specs=pl.BlockSpec(memory_space=pltpu.VMEM),
        scratch_shapes=scratch,
        compiler_params=pltpu.CompilerParams(
            collective_id=0, has_side_effects=True, vmem_limit_bytes=60 * 1024 * 1024
        ),
        cost_estimate=pl.CostEstimate(
            flops=13_000_000_000, bytes_accessed=8_000_000, transcendentals=17_000_000
        ),
    )(
        hidden_in, norm_gain, w_query, enc_states, w_key, w_value, w_out, block_counts
    )


def solution(mesh):
    placed = (
        P(("dp", "span"), "head"),
        P("head"),
        P(None, "head"),
        P(("dp", "span", "head"), None),
        P(None, "head"),
        P(None, "head"),
        P("head", None),
        P("dp"),
    )
    return jax.shard_map(
        per_device, mesh=mesh, in_specs=placed, out_specs=P(("dp", "span"), "head"), check_vma=False
    )
```

```python
import math

import jax
import jax.numpy as jnp
from jax import lax
from jax.experimental import pallas as pl
from jax.experimental.pallas import tpu as pltpu
from jax.sharding import PartitionSpec as P

HD = 128
X = 4
Y = 4
Z = 8
HEAD = X * Y
T = 256
CHUNKS = 2
F = 256
BLOCK = 128
SLOTS = 16
KEYS = BLOCK * SLOTS
TILE = 256
FIRST = 0
BLOCK_ORDER = (0, 1, 2, 8, 9, 10, 3, 4, 11, 12, 5, 6, 13, 14, 7, 15)
DE = 1024
LOG2E = 1.4426950408889634
COEF = LOG2E / math.sqrt(HD)
NEG = -1e30
F32 = jnp.float32
BF16 = jnp.bfloat16
MESH = pl.DeviceIdType.MESH


def div(value, by):
    return value // by if isinstance(value, int) else lax.div(value, by)


def rem(value, by):
    return value % by if isinstance(value, int) else lax.rem(value, by)


def wrap(value, size):
    return rem(value + 2 * size, size)


class Place:
    def __init__(self):
        self.dp = lax.axis_index("dp")
        self.z = lax.axis_index("span")
        self.head = lax.axis_index("head")
        self.x = div(self.head, Y)
        self.y = rem(self.head, Y)

    def slot(self, dx, dy):
        return wrap(self.x + dx, X) * Y + wrap(self.y + dy, Y)

    def at_xy(self, dx, dy):
        return (self.dp, self.z, self.slot(dx, dy))

    def at_z(self, dz):
        return (self.dp, wrap(self.z + dz, Z), self.head)


class Gather:
    REL = (0, -1, 1, 2)

    def __init__(self, place, buf, rows, send, recv):
        self.place, self.buf, self.rows, self.send, self.recv = place, buf, rows, send, recv
        self.started = []

    def shift(self, half, da, db):
        return (db, da) if half == 0 else (da, db)

    def part(self, half, da, db, quarter):
        base = half * (self.rows // 2)
        count = self.rows // 2
        if quarter is not None:
            count = self.rows // 4
            base = base + quarter * count
        return self.buf.at[self.place.slot(*self.shift(half, da, db)), pl.ds(base, count)]

    def copy(self, half, index, ref, to):
        return pltpu.make_async_remote_copy(
            src_ref=ref,
            dst_ref=ref,
            send_sem=self.send.at[half * 20 + index],
            recv_sem=self.recv.at[half * 20 + index],
            device_id=to,
            device_id_type=MESH,
        )

    def sent(self, half, index, da, db, quarter, ta, tb):
        ref = self.part(half, da, db, quarter)
        return self.copy(half, index, ref, self.place.at_xy(*self.shift(half, ta, tb)))

    def go(self, *what):
        self.sent(*what).start()
        self.started.append(what)

    def take(self, half, index, da, db, quarter):
        ref = self.part(half, da, db, quarter)
        self.copy(half, index, ref, self.place.at_xy(1, 0)).wait_recv()

    def line(self, half, which):
        base = 4 + 4 * which
        rel = self.REL[which]
        self.go(half, base, rel, 0, None, 0, 1)
        self.go(half, base + 1, rel, 0, None, 0, -1)

    def pass_on(self, half, which):
        base = 4 + 4 * which
        rel = self.REL[which]
        self.take(half, base, rel, -1, None)
        self.go(half, base + 2, rel, -1, 0, 0, 1)
        self.take(half, base + 1, rel, 1, None)
        self.go(half, base + 3, rel, 1, 1, 0, -1)

    def s0(self):
        for half in range(2):
            self.go(half, 0, 0, 0, None, 1, 0)
            self.go(half, 1, 0, 0, None, -1, 0)
        for half in range(2):
            self.line(half, 0)

    def s1(self):
        for half in range(2):
            self.take(half, 0, -1, 0, None)
            self.go(half, 2, -1, 0, 0, 1, 0)
            self.take(half, 1, 1, 0, None)
            self.go(half, 3, 1, 0, 1, -1, 0)
        for half in range(2):
            self.line(half, 1)
            self.line(half, 2)

    def s2(self):
        for half in range(2):
            self.pass_on(half, 0)

    def s3(self):
        for half in range(2):
            self.take(half, 2, 2, 0, 0)
            self.take(half, 3, 2, 0, 1)
            self.line(half, 3)

    def s4(self):
        for which in (1, 2):
            for half in range(2):
                self.pass_on(half, which)

    def s5(self):
        for half in range(2):
            self.pass_on(half, 3)

    def s6(self):
        for which in range(4):
            for half in range(2):
                base = 4 + 4 * which
                rel = self.REL[which]
                self.take(half, base + 2, rel, 2, 0)
                self.take(half, base + 3, rel, 2, 1)

    def finish(self):
        for what in self.started:
            self.sent(*what).wait_send()


class QueryRing:
    def __init__(self, place, buf, chunk, send, recv):
        self.place, self.buf, self.chunk, self.send, self.recv = place, buf, chunk, send, recv
        self.started = []

    def copy(self, way, step, head, dz):
        ref = self.buf.at[self.chunk, wrap(self.place.z + dz, Z), pl.ds(head * HD, HD)]
        index = ((self.chunk * 2 + way) * 4 + step) * 2 + head
        return pltpu.make_async_remote_copy(
            src_ref=ref,
            dst_ref=ref,
            send_sem=self.send.at[index],
            recv_sem=self.recv.at[index],
            device_id=self.place.at_z(1 - 2 * way),
            device_id_type=MESH,
        )

    def go(self, way, step, head):
        if step == 3 and head != way:
            return
        what = (way, step, head, -step if way == 0 else step)
        self.copy(*what).start()
        self.started.append(what)

    def begin(self):
        for head in range(2):
            for way in range(2):
                self.go(way, 0, head)

    def hop(self, step):
        for head in range(2):
            for way in range(2):
                if step == 3 and head != way:
                    continue
                self.copy(way, step, head, -1 - step if way == 0 else 1 + step).wait_recv()
                if step < 3:
                    self.go(way, step + 1, head)

    def finish(self):
        for what in self.started:
            self.copy(*what).wait_send()


def kernel(
    hidden_hbm, gain_ref, wq_hbm, enc_hbm, wk_hbm, wv_hbm, wo_hbm, count_ref, out_ref,
    wq, wk, wv, wo, nbuf, ebuf, qbuf, kbuf, vbuf, score_0, score_1, best_0, best_1, blocks_o, blocks_s, live_buf,

    osend, orecv, attb,
    st1, rv1, st2, rv2, st3, rv3, parts, gains,
    local_sem, ms_ss, ms_rs, ag_ss, ag_rs, q_ss, q_rs, o_ss, o_rs, x_ss, x_rs,
):
    place = Place()
    me = place.head
    z = place.z

    local = [
        pltpu.make_async_copy(source, target, local_sem.at[index])
        for index, (source, target) in enumerate(
            (
                (hidden_hbm.at[pl.ds(0, T)], nbuf.at[0, me]),
                (hidden_hbm.at[pl.ds(T, T)], nbuf.at[1, me]),
                (enc_hbm, ebuf.at[me]),
                (wq_hbm, wq),
                (wk_hbm, wk),
                (wv_hbm, wv),
                (wo_hbm, wo),
            )
        )
    ]
    for copy in local:
        copy.start()

    barrier = pltpu.get_barrier_semaphore()
    partners = [place.at_xy(d, 0) for d in (1, 2, 3)]
    partners += [place.at_xy(0, d) for d in (1, 2, 3)]
    partners += [place.at_z(d) for d in (1, -1, 2, -2)]
    for partner in partners:
        pl.semaphore_signal(barrier, inc=1, device_id=partner, device_id_type=MESH)

    gains[pl.ds(me, 1)] = jnp.broadcast_to(gain_ref[...].astype(F32).reshape(1, 1, F), (1, 8, F))

    def gain_copy(stage, d, behind=0):
        if stage == 0:
            ref, to = gains.at[place.slot(0, -behind)], place.at_xy(0, d)
        else:
            ref, to = gains.at[pl.ds(wrap(place.x - behind, X) * Y, Y)], place.at_xy(d, 0)
        return pltpu.make_async_remote_copy(
            src_ref=ref,
            dst_ref=ref,
            send_sem=ms_ss.at[stage * 3 + d - 1],
            recv_sem=ms_rs.at[stage * 3 + d - 1],
            device_id=to,
            device_id_type=MESH,
        )

    def gain_go(stage):
        for d in (1, 2, 3):
            gain_copy(stage, d).start()

    def gain_take(stage):
        for d in (1, 2, 3):
            gain_copy(stage, d, d).wait_recv()

    gather_e = Gather(place, ebuf, BLOCK, ag_ss.at[0], ag_rs.at[0])
    gather_a = Gather(place, nbuf.at[0], T, ag_ss.at[1], ag_rs.at[1])
    gather_b = Gather(place, nbuf.at[1], T, ag_ss.at[2], ag_rs.at[2])
    ring_a = QueryRing(place, qbuf, 0, q_ss, q_rs)
    ring_b = QueryRing(place, qbuf, 1, q_ss, q_rs)

    def project(chunk):
        squares = jnp.zeros((T, F), F32)
        for source in range(HEAD):
            rows = nbuf[chunk, source].astype(F32)
            squares = squares + rows * rows
        mean = jnp.sum(squares, axis=1, keepdims=True) * (1.0 / (HEAD * F))
        inverse = lax.rsqrt(mean + 1e-05)
        acc = jnp.zeros((T, F), F32)
        for source in range(HEAD):
            rows = nbuf[chunk, source].astype(F32) * inverse * gains[source, 0:1, :]
            acc = acc + jnp.dot(
                rows.astype(BF16), wq[source * F : (source + 1) * F], preferred_element_type=F32
            )
        qbuf[chunk, pl.ds(z, 1)] = acc.T.astype(BF16)[None]

    live_blocks = count_ref[z]

    def encode():
        for part in range(4):
            rows = ebuf[4 * part : 4 * part + 4].reshape(4 * BLOCK, DE)
            keys = jnp.dot(rows, wk[...], preferred_element_type=F32)
            values = jnp.dot(rows, wv[...], preferred_element_type=F32)
            slot = lax.broadcasted_iota(jnp.int32, (4 * BLOCK, HD), 0) // BLOCK + 4 * part
            live = slot < live_blocks
            span = pl.ds(part * 4 * BLOCK, 4 * BLOCK)
            for head in range(2):
                cols = slice(head * HD, (head + 1) * HD)
                key_block = keys[:, cols]
                lead = key_block[:BLOCK] if part == 0 else kbuf[head, :BLOCK].astype(F32)
                lead = jnp.concatenate([lead] * 4, axis=0)
                kbuf[head, span] = jnp.where(live, key_block, lead).astype(BF16)
                vbuf[cols, span] = jnp.where(live, values[:, cols], 0.0).T.astype(BF16)

    blocks_s[...] = jnp.zeros((CHUNKS * Z, 8, T), F32)
    for slot in range(SLOTS):
        alive = (jnp.zeros((8, T), jnp.int32) + slot) < live_blocks
        live_buf[slot] = jnp.where(alive, 1.0, 0.0)

    pl.semaphore_wait(barrier, len(partners))
    local[0].wait()
    gather_a.s0()
    local[1].wait()
    gather_b.s0()
    gain_go(0)
    gather_a.s1()
    gather_a.s2()
    gain_take(0)
    gain_go(1)
    gather_a.s3()
    gather_b.s1()
    gather_a.s4()
    gather_a.s5()
    gather_b.s2()
    gather_b.s3()
    gather_a.s6()
    gain_take(1)
    local[3].wait()
    project(0)
    ring_a.begin()
    gather_b.s4()
    gather_b.s5()
    local[2].wait()
    gather_e.s0()
    ring_a.hop(0)
    gather_b.s6()
    project(1)
    ring_b.begin()
    ring_a.hop(1)
    gather_e.s1()
    ring_b.hop(0)
    gather_e.s2()
    gather_e.s3()
    ring_a.hop(2)
    ring_b.hop(1)
    gather_e.s4()
    ring_a.hop(3)
    ring_b.hop(2)
    gather_e.s5()
    ring_b.hop(3)
    gather_e.s6()
    local[4].wait()
    local[5].wait()
    encode()
    local[6].wait()

    score_buf = (score_0, score_1)
    best_buf = (best_0, best_1)

    def sides(i):
        step = div(i + 1, 2)
        way = rem(i + 1, 2)
        return step, way, wrap(z + (1 - 2 * way) * (4 - step), Z)

    def phase(soft, soft_head, block, head):
        if block is not None:
            query = qbuf[div(block, 8), sides(rem(block, 8))[2], pl.ds(head * HD, HD), :]
            top = None
        if soft is not None:
            best = best_buf[soft_head][0:1, :]
            acc = jnp.zeros((HD, T), F32)
            total = jnp.zeros((8, T), F32)
        for tile in range(KEYS // TILE):
            span = slice(tile * TILE, (tile + 1) * TILE)
            if block is not None:
                scores = jnp.dot(kbuf[head, span], query, preferred_element_type=F32)
                score_buf[head][span] = scores
                peak = jnp.max(scores.reshape(TILE // 8, 8, T), axis=0)
                top = peak if top is None else jnp.maximum(top, peak)
            if soft is not None:
                weights = jnp.exp2(score_buf[soft_head][span] * COEF - best)
                for inner in range(TILE // BLOCK):
                    rows = weights[inner * BLOCK : (inner + 1) * BLOCK]
                    rows = jnp.sum(rows.reshape(BLOCK // 8, 8, T), axis=0)
                    total = total + rows * live_buf[tile * (TILE // BLOCK) + inner]
                acc = acc + jnp.dot(
                    vbuf[soft_head * HD : (soft_head + 1) * HD, span],
                    weights.astype(BF16),
                    preferred_element_type=F32,
                )
        if block is not None:
            top = jnp.max(top, axis=0, keepdims=True) * COEF
            best_buf[head][...] = jnp.broadcast_to(top, (8, T))
        if soft is not None:
            blocks_o[soft, pl.ds(soft_head * HD, HD)] = acc
            blocks_s[soft, pl.ds(2 * soft_head, 1)] = best
            blocks_s[soft, pl.ds(2 * soft_head + 1, 1)] = jnp.sum(total, axis=0, keepdims=True)

    def split3(value):
        high = value.astype(BF16).astype(F32)
        middle = (value - high).astype(BF16).astype(F32)
        return [high, middle, value - high - middle]

    def o_copy(chunk, way, step, head):
        index = ((chunk * 2 + way) * 4 + step) * 2 + head
        return pltpu.make_async_remote_copy(
            src_ref=osend.at[chunk, way, step, head],
            dst_ref=orecv.at[chunk, way, step, head],
            send_sem=o_ss.at[index],
            recv_sem=o_rs.at[index],
            device_id=(place.dp, wrap(z + (1 - 2 * way) * (2 if step is FIRST else 1), Z), place.head),
            device_id_type=MESH,
        )

    def held(block, head):
        return (
            blocks_o[block, pl.ds(head * HD, HD), :],
            blocks_s[block, pl.ds(2 * head, 1), :],
            blocks_s[block, pl.ds(2 * head + 1, 1), :],
        )

    def send_part(chunk, way, step, head, part):
        values, best, total = part
        osend[chunk, way, step, head, :HD] = values.astype(BF16)
        rows = split3(best) + split3(total) + [jnp.zeros((10, T), F32)]
        osend[chunk, way, step, head, HD:] = jnp.concatenate(rows, axis=0).astype(BF16)
        o_copy(chunk, way, step, head).start()

    def merge_part(chunk, way, step, head, part):
        o_copy(chunk, way, step, head).wait_recv()
        values, best_a, total = part
        stats = orecv[chunk, way, step, head, HD:, :].astype(F32)
        best_b = stats[0:1] + stats[1:2] + stats[2:3]
        total_b = stats[3:4] + stats[4:5] + stats[5:6]
        best = jnp.maximum(best_a, best_b)
        scale_a = jnp.exp2(best_a - best)
        scale_b = jnp.exp2(best_b - best)
        values = values * scale_a + orecv[chunk, way, step, head, :HD, :].astype(F32) * scale_b
        return values, best, total * scale_a + total_b * scale_b

    def out_axes(half, da, db):
        return (da, db) if half == 0 else (db, da)

    def out_copy(chunk, half, way, step, db=0):
        if step < 2:
            send, recv = ((st1, rv1), (st2, rv2))[step]
            source, target = send.at[chunk, half, way, db], recv.at[chunk, half, way, db]
            to = place.at_xy(*out_axes(half, 1 - 2 * way, 0))
            index = ((chunk * 2 + half) * 2 + way) * 8 + step * 4 + db
        else:
            source, target = st3.at[chunk, half, db - 1], rv3.at[chunk, half, db - 1]
            to = place.at_xy(*out_axes(half, 0, db))
            index = CHUNKS * 32 + (chunk * 2 + half) * 3 + db - 1
        return pltpu.make_async_remote_copy(
            src_ref=source,
            dst_ref=target,
            send_sem=x_ss.at[index],
            recv_sem=x_rs.at[index],
            device_id=to,
            device_id_type=MESH,
        )

    def out_part(chunk, half, da, db):
        slot = place.slot(*out_axes(half, da, db))
        return jnp.dot(
            attb[chunk, half * 128 : (half + 1) * 128],
            wo[:, pl.ds(pl.multiple_of(slot * F, F), F)],
            preferred_element_type=F32,
        )

    ORDER = (2, 1, 3, 0)

    def out_1(chunk):
        for db in ORDER:
            for half in range(2):
                part = out_part(chunk, half, 2, db).astype(BF16)
                for way in range(2):
                    st1[chunk, half, way, db] = part[64 * way : 64 * way + 64]
                    out_copy(chunk, half, way, 0, db).start()
    def out_rest(chunk):
        for da in (1, 3, 0):
            for db in ORDER:
                for half in range(2):
                    parts[chunk, half, da, db] = out_part(chunk, half, da, db)

    def out_2(chunk):
        for db in ORDER:
            for half in range(2):
                for way in range(2):
                    same = slice(64 * way, 64 * way + 64)
                    rest = slice(64 - 64 * way, 128 - 64 * way)
                    da = (1, 3)[way]
                    st2[chunk, half, way, db, rest] = parts[chunk, half, da, db, rest].astype(BF16)
                    out_copy(chunk, half, way, 0, db).wait_recv()
                    part = parts[chunk, half, da, db, same] + rv1[chunk, half, way, db].astype(F32)
                    st2[chunk, half, way, db, same] = part.astype(BF16)
                    out_copy(chunk, half, way, 1, db).start()

    def out_3(chunk):
        for db in ORDER:
            for half in range(2):
                part = parts[chunk, half, 0, db]
                for way in range(2):
                    out_copy(chunk, half, way, 1, db).wait_recv()
                    part = part + rv2[chunk, half, way, db].astype(F32)
                if db > 0:
                    st3[chunk, half, db - 1] = part.astype(BF16)
                    out_copy(chunk, half, 0, 2, db).start()
                else:
                    parts[chunk, half, 0, 0] = part

    def out_4(chunk):
        for half in range(2):
            part = parts[chunk, half, 0, 0]
            for db in (1, 3, 2):
                out_copy(chunk, half, 0, 2, db).wait_recv()
                part = part + rv3[chunk, half, db - 1].astype(F32)
            start = chunk * T + half * 128
            out_ref[start : start + 128] = part.astype(BF16)

    def number(m):
        block = BLOCK_ORDER[0]
        for at in range(1, 16):
            block = block + div(m + 16 - at, 16) * (BLOCK_ORDER[at] - BLOCK_ORDER[at - 1])
        return block

    def send_first(block, head):
        i = rem(block, 8)
        chunk = div(block, 8)
        pl.when(i == 0)(lambda: send_part(chunk, head, FIRST, head, held(block, head)))
        pl.when(jnp.logical_and(i > 0, i < 3))(
            lambda: send_part(chunk, rem(i + 1, 2), 1, head, held(block, head))
        )

    def pass_on(chunk, block, step, way, head):
        both = jnp.logical_and(step == 2, way == head)

        @pl.when(both)
        def _():
            part = merge_part(chunk, way, FIRST, head, held(block, head))
            part = merge_part(chunk, way, 1, head, part)
            send_part(chunk, way, 2, head, part)

        @pl.when(jnp.logical_not(both))
        def _():
            part = merge_part(chunk, way, step - 1, head, held(block, head))
            send_part(chunk, way, step, head, part)

    def complete(chunk, block, head):
        part = held(block, head)
        for way in range(2):
            part = merge_part(chunk, way, 3, head, part)
        attb[chunk, :, pl.ds(head * HD, HD)] = (part[0] / part[2]).T.astype(BF16)

    def return_part(m, head):
        block = number(m)
        chunk, i = div(block, 8), rem(block, 8)
        step, way, _ = sides(i)
        inner = jnp.logical_and(i > 2, i < 7)
        pl.when(inner)(lambda: pass_on(chunk, block, step, way, head))
        pl.when(i == 7)(lambda: complete(chunk, block, head))

    def gain_finish():
        for stage in range(2):
            for d in (1, 2, 3):
                gain_copy(stage, d).wait_send()

    def one_block(m, carry):
        now, later = number(m), number(rem(m + 1, 16))
        phase(now, 0, now, 1)
        send_first(now, 0)
        pl.when(m > 0)(lambda: return_part(m - 1, 0))
        phase(now, 1, later, 0)
        send_first(now, 1)
        pl.when(m > 0)(lambda: return_part(m - 1, 1))
        pl.when(m == 15)(lambda: out_1(0))
        pl.when(m == 15)(lambda: out_rest(0))
        for at, work in (
            (2, gather_a.finish),
            (3, gather_b.finish),
            (4, gather_e.finish),
            (5, ring_a.finish),
            (6, ring_b.finish),
            (7, gain_finish),
        ):
            pl.when(m == at)(work)
        return carry

    phase(None, 0, 0, 0)
    lax.fori_loop(0, 8 * CHUNKS, one_block, 0)
    for head in range(2):
        complete(1, 15, head)
    out_1(1)
    out_2(0)
    out_rest(1)
    out_2(1)
    out_3(0)
    out_3(1)
    out_4(0)
    out_4(1)

    for chunk in range(CHUNKS):
        for way in range(2):
            for step in range(4):
                for half in range(2):
                    if step > 0 or half == way:
                        o_copy(chunk, way, step, half).wait_send()
                    for db in range(4):
                        if step < 2 or (step == 2 and way == 0 and db > 0):
                            out_copy(chunk, half, way, step, db).wait_send()


def per_device(hidden_in, norm_gain, w_query, enc_states, w_key, w_value, w_out, block_counts):
    any_spec = pl.BlockSpec(memory_space=pl.ANY)
    vmem = pltpu.VMEM
    dma = pltpu.SemaphoreType.DMA
    scratch = [
        vmem((HEAD * F, F), BF16),
        vmem((DE, F), BF16),
        vmem((DE, F), BF16),
        vmem((F, HEAD * F), BF16),
        vmem((CHUNKS, HEAD, T, F), BF16),
        vmem((HEAD, BLOCK, DE), BF16),
        vmem((CHUNKS, Z, F, T), BF16),
        vmem((2, KEYS, HD), BF16),
        vmem((F, KEYS), BF16),
        vmem((KEYS, T), F32),
        vmem((KEYS, T), F32),
        vmem((8, T), F32),
        vmem((8, T), F32),
        vmem((CHUNKS * Z, F, T), F32),
        vmem((CHUNKS * Z, 8, T), F32),
        vmem((SLOTS, 8, T), F32),
        vmem((CHUNKS, 2, 4, 2, HD + 16, T), BF16),
        vmem((CHUNKS, 2, 4, 2, HD + 16, T), BF16),
        vmem((CHUNKS, T, F), BF16),
        vmem((CHUNKS, 2, 2, 4, 64, F), BF16),
        vmem((CHUNKS, 2, 2, 4, 64, F), BF16),
        vmem((CHUNKS, 2, 2, 4, 128, F), BF16),
        vmem((CHUNKS, 2, 2, 4, 128, F), BF16),
        vmem((CHUNKS, 2, 3, 128, F), BF16),
        vmem((CHUNKS, 2, 3, 128, F), BF16),
        vmem((CHUNKS, 2, 4, 4, 128, F), F32),
        vmem((HEAD, 8, F), F32),
        dma((7,)),
        dma((6,)),
        dma((6,)),
        dma((3, 40)),
        dma((3, 40)),
        dma((CHUNKS * 16,)),
        dma((CHUNKS * 16,)),
        dma((CHUNKS * 16,)),
        dma((CHUNKS * 16,)),
        dma((CHUNKS * 38,)),
        dma((CHUNKS * 38,)),
    ]
    return pl.pallas_call(
        kernel,
        out_shape=pltpu.VMEM((CHUNKS * T, F), BF16),
        in_specs=[
            any_spec,
            pl.BlockSpec(memory_space=pltpu.VMEM),
            any_spec,
            any_spec,
            any_spec,
            any_spec,
            any_spec,
            pl.BlockSpec(memory_space=pltpu.SMEM),
        ],
        out_specs=pl.BlockSpec(memory_space=pltpu.VMEM),
        scratch_shapes=scratch,
        compiler_params=pltpu.CompilerParams(
            collective_id=0, has_side_effects=True, vmem_limit_bytes=60 * 1024 * 1024
        ),
        cost_estimate=pl.CostEstimate(
            flops=13_000_000_000, bytes_accessed=8_000_000, transcendentals=17_000_000
        ),
    )(
        hidden_in, norm_gain, w_query, enc_states, w_key, w_value, w_out, block_counts
    )


def solution(mesh):
    placed = (
        P(("dp", "span"), "head"),
        P("head"),
        P(None, "head"),
        P(("dp", "span", "head"), None),
        P(None, "head"),
        P(None, "head"),
        P("head", None),
        P("dp"),
    )
    return jax.shard_map(
        per_device, mesh=mesh, in_specs=placed, out_specs=P(("dp", "span"), "head"), check_vma=False
    )
```
